256 devices in a mesh: dp: 4 (over y), space: 32 (over x_lo, z, core), tensor: 2 (over x_hi).
Axes of the slice: x: 4 (x_hi: 2, x_lo: 2; x = x_hi * 2 + x_lo), y: 4, z: 8, core: 2. Of those that a mesh axis runs over, the one named last changes fastest.
Arguments:
- queries: bfloat16 [4, 16, 256, 5120], P('dp', None, 'space', 'tensor'), may hold values from -60 to 60, as said below
- keys: bfloat16 [4, 16, 256, 5120], P('dp', None, 'space', 'tensor'), may hold values from -4 to 4
- values: bfloat16 [4, 16, 256, 5120], P('dp', None, 'space', 'tensor'), may hold values from -6 to 6
- cotangent: bfloat16 [4, 16, 256, 5120], P('dp', None, 'space', 'tensor'), may hold values from -6 to 6
- land: int32 [16, 256], replicated, may hold values 0 or 1
- shifts: int32 [2], replicated, may hold values from 1 to 7
- bias_network_first_weight: float32 [2, 512], replicated, may hold values from -4 to 4
- bias_network_first_offset: float32 [512], replicated, may hold values from -3 to 3
- bias_network_second_weight: float32 [512, 40], P(None, 'tensor'), may hold values from -0.25 to 0.25
- surface_key_bias: float32 [2, 40], P(None, 'tensor'), may hold values from -4 to 4
Outputs:
- grad_queries: bfloat16 [4, 16, 256, 5120], P('dp', None, 'space', 'tensor')
- grad_keys: bfloat16 [4, 16, 256, 5120], P('dp', None, 'space', 'tensor')
- grad_values: bfloat16 [4, 16, 256, 5120], P('dp', None, 'space', 'tensor')
- grad_first: float32 [2, 512], replicated
- grad_first_bias: float32 [512], replicated
- grad_second: float32 [512, 40], P(None, 'tensor')
- grad_key_bias: float32 [2, 40], P(None, 'tensor')
The draws below stay inside these ranges and needn't reach their ends.
Inputs may be any that keep to these rules, and one draw needn't show every extreme that they name: queries: in the hidden draw some queries are aligned with their own key. shifts[0] is the latitude offset, shifts[1] the longitude offset.
All inputs are finite; a program needn't handle non-finite values.
Results may differ from the reference program's by a relative error of at most 0.02.
Values may be sent and summed in bfloat16 or wider, within the bound.
A program may use at most 128 MiB of HBM per device.

```python
import jax
import jax.numpy as jnp
from jax import lax

ATTENTION_HEADS = 40
HD = 128
BIAS_NET_HIDDEN = 512
LAT = 16
LON = 256
DATES = 4


def shared_normal(key):
    return jax.random.normal(key, (DATES, LAT, LON, ATTENTION_HEADS * HD), jnp.float32)


def draw_keys(key, part):
    base = shared_normal(key)
    return jnp.clip(base, -4.0, 4.0).astype(jnp.bfloat16)


def draw_queries(key, part):
    key = jax.random.fold_in(key, 5)
    first_key = jax.random.fold_in(key, 0)
    shape = (DATES, LAT, LON, ATTENTION_HEADS * HD)
    drawn = jax.random.normal(first_key, shape, jnp.float32)
    return jnp.clip(drawn, -6.0, 6.0).astype(jnp.bfloat16)


def with_ends(result, rng, least, high):
    dims = result.shape
    place = [jax.random.randint(jax.random.fold_in(rng, axis), (), 0, dims[axis]) for axis in range(len(dims))]
    result = result.at[tuple(place)].set(least)
    longest = dims.index(max(dims))
    place[longest] = (place[longest] + 1) % dims[longest]
    return result.at[tuple(place)].set(high)


def shard_levels(stream_key, dims, cuts, low, high):
    gain, own = 1.0, jax.random.fold_in(stream_key, 6)
    for axis_at, blocks in cuts:
        draws = jnp.exp(jax.random.uniform(jax.random.fold_in(own, axis_at), (blocks,), jnp.float32, low / len(cuts), high / len(cuts)))
        gain = gain * jnp.repeat(draws, dims[axis_at] // blocks).reshape([-1 if axis == axis_at else 1 for axis in range(len(dims))])
    return gain


def bell_draw(stream_key, dims, deviation, bound, cuts=(), held_as=jnp.bfloat16):
    gain = shard_levels(stream_key, dims, cuts, -0.22, 0.18) if cuts else 1.0
    result = jax.random.normal(stream_key, dims, jnp.float32) * deviation * gain
    return jnp.minimum(jnp.maximum(result, -bound), bound).astype(held_as)


def setup_inputs(seed: int = 0) -> dict:
    key_list = jax.random.split(jax.random.key(seed), 11)
    queries = draw_queries(jax.random.fold_in(key_list[10], 71), 0)
    keys = draw_keys(jax.random.fold_in(key_list[10], 71), 0)
    values = bell_draw(key_list[2], (DATES, LAT, LON, ATTENTION_HEADS * HD), 1.0, 6.0, ((0, 4), (2, 32), (3, 2)))
    cotangent = bell_draw(key_list[3], (DATES, LAT, LON, ATTENTION_HEADS * HD), 1.0, 6.0, ((0, 4), (2, 32), (3, 2)))
    land = with_ends((jax.random.randint(key_list[4], (LAT, LON), 0, 5) < 2).astype(jnp.int32), jax.random.fold_in(key_list[4], 1), 0, 1)
    shifts = jax.random.randint(key_list[5], (2,), 1, 8).astype(jnp.int32)
    bias_network_first_weight = bell_draw(key_list[6], (2, BIAS_NET_HIDDEN), 2 ** -0.5, 4.0, (), jnp.float32)
    bias_network_first_offset = bell_draw(key_list[7], (BIAS_NET_HIDDEN,), 0.5, 3.0, (), jnp.float32)
    bias_network_second_weight = bell_draw(key_list[8], (BIAS_NET_HIDDEN, ATTENTION_HEADS), BIAS_NET_HIDDEN ** -0.5, 0.25, ((1, 2),), jnp.float32)
    surface_key_bias = bell_draw(key_list[9], (2, ATTENTION_HEADS), 1.0, 4.0, ((1, 2),), jnp.float32)
    return dict(queries=queries, keys=keys, values=values, cotangent=cotangent, land=land, shifts=shifts, bias_network_first_weight=bias_network_first_weight, bias_network_first_offset=bias_network_first_offset, bias_network_second_weight=bias_network_second_weight, surface_key_bias=surface_key_bias)


MASKED = -1000000000.0

def squash(t):
    return jnp.sign(t) * jnp.log2(1.0 + jnp.abs(t)) / 3.0

def position_table_bias(first, first_bias, second):
    pos = jnp.arange(64, dtype=jnp.int32)
    rowpos = (pos // 8).astype(jnp.float32)
    colpos = (pos % 8).astype(jnp.float32)
    coords = jnp.stack([squash(rowpos[:, None] - rowpos[None, :]), squash(colpos[:, None] - colpos[None, :])], -1).reshape(4096, 2)
    hidden = jax.nn.relu(jnp.dot(coords, first, precision=lax.Precision.HIGHEST) + first_bias)
    logits = jnp.dot(hidden, second, precision=lax.Precision.HIGHEST)
    return jnp.transpose((16.0 * jax.nn.sigmoid(logits)).reshape(64, 64, -1), (2, 0, 1))

def to_windows(field, shift_lat, heads):
    dates, lat, cols, chans = field.shape
    rows = 8 * (lat // 8 + 1)
    padded = jnp.pad(field, ((0, 0), (8, 8), (0, 0), (0, 0)))
    part = lax.dynamic_slice_in_dim(padded, shift_lat, rows, 1)
    part = part.reshape(dates, rows // 8, 8, cols // 8, 8, heads, chans // heads)
    return part.transpose(0, 1, 3, 2, 4, 5, 6).reshape(-1, 64, heads, chans // heads)

def from_windows(windows, shift_lat, shape):
    dates, lat, cols, chans = shape
    rows = 8 * (lat // 8 + 1)
    heads = windows.shape[2]
    part = windows.reshape(dates, rows // 8, cols // 8, 8, 8, heads, chans // heads)
    part = part.transpose(0, 1, 3, 2, 4, 5, 6).reshape(dates, rows, cols, chans)
    padded = jnp.zeros((dates, lat + 16, cols, chans), windows.dtype)
    padded = lax.dynamic_update_slice_in_dim(padded, part, shift_lat, 1)
    return padded[:, 8:8 + lat]

def window_grads(queries, keys, values, cotangent, land, position_table, surface_key_bias, shift_lat):
    heads = position_table.shape[0]
    shape = queries.shape
    scale = (shape[3] // heads) ** (-0.5)
    qwin = to_windows(queries, shift_lat, heads).astype(jnp.float32)
    kwin = to_windows(keys, shift_lat, heads).astype(jnp.float32)
    vwin = to_windows(values, shift_lat, heads).astype(jnp.float32)
    dwin = to_windows(cotangent, shift_lat, heads).astype(jnp.float32)
    ones = jnp.ones((shape[0], shape[1], shape[2], 1), jnp.float32)
    landf = jnp.broadcast_to(land.astype(jnp.float32)[None, :, :, None], ones.shape)
    valid = to_windows(ones, shift_lat, 1)[:, :, 0, 0]
    landw = to_windows(landf, shift_lat, 1)[:, :, 0, 0]
    keyterm = surface_key_bias[0][None, :, None] + (surface_key_bias[1] - surface_key_bias[0])[None, :, None] * landw[:, None, :] + MASKED * (1.0 - valid)[:, None, :]
    scores = jnp.einsum('wihd,wjhd->whij', qwin, kwin) * scale + position_table[None] + keyterm[:, :, None, :]
    probs = jax.nn.softmax(scores, axis=-1)
    probs_low = probs.astype(jnp.bfloat16).astype(jnp.float32)
    grad_v = jnp.einsum('whij,wihd->wjhd', probs_low, dwin)
    dprobs = jnp.einsum('wihd,wjhd->whij', dwin, vwin)
    delta = lax.optimization_barrier(jnp.sum(probs * dprobs, axis=-1, keepdims=True))
    dscores = probs * (dprobs - delta)
    dlow = dscores.astype(jnp.bfloat16).astype(jnp.float32)
    grad_q = jnp.einsum('whij,wjhd->wihd', dlow, kwin) * scale
    grad_k = jnp.einsum('whij,wihd->wjhd', dlow, qwin) * scale
    table_grad = lax.optimization_barrier(jnp.sum(dscores, axis=0))
    column_sums = lax.optimization_barrier(jnp.sum(dscores, axis=2))
    land_part = jnp.einsum('whj,wj->h', column_sums, landw)
    every = lax.optimization_barrier(jnp.sum(column_sums, axis=(0, 2)))
    key_grad = jnp.stack([every - land_part, land_part])
    return (from_windows(grad_q, shift_lat, shape), from_windows(grad_k, shift_lat, shape), from_windows(grad_v, shift_lat, shape), table_grad, key_grad)

def reference(queries, keys, values, cotangent, land, shifts, bias_network_first_weight, bias_network_first_offset, bias_network_second_weight, surface_key_bias):
    position_table = position_table_bias(bias_network_first_weight, bias_network_first_offset, bias_network_second_weight)
    shift_lat = shifts[0]
    shift_lon = shifts[1]
    land_rolled = jnp.roll(land, -shift_lon, axis=1)
    rolled = [jnp.roll(a, -shift_lon, axis=2) for a in (queries, keys, values, cotangent)]
    grads_q, grads_k, grads_v = ([], [], [])
    table_grad = jnp.zeros(position_table.shape, jnp.float32)
    key_grad = jnp.zeros(surface_key_bias.shape, jnp.float32)
    for date in range(DATES):
        pieces = [a[date:date + 1] for a in rolled]
        out = window_grads(pieces[0], pieces[1], pieces[2], pieces[3], land_rolled, position_table, surface_key_bias, shift_lat)
        grads_q.append(out[0])
        grads_k.append(out[1])
        grads_v.append(out[2])
        table_grad = table_grad + out[3]
        key_grad = key_grad + out[4]
    back = [jnp.roll(jnp.concatenate(g, axis=0), shift_lon, axis=2).astype(jnp.bfloat16) for g in (grads_q, grads_k, grads_v)]
    ignored_value, gather_pull = jax.vjp(position_table_bias, bias_network_first_weight, bias_network_first_offset, bias_network_second_weight)
    grad_first, grad_first_bias, grad_second = gather_pull(table_grad)
    return (back[0], back[1], back[2], grad_first, grad_first_bias, grad_second, key_grad)
```

```python
import functools

import jax
import jax.numpy as jnp
from jax import lax
from jax.experimental import pallas as pl
from jax.experimental.pallas import tpu as pltpu
from jax.sharding import PartitionSpec as P

MESH = pl.DeviceIdType.MESH
MASKED = -1000000000.0
LOG2E = 1.4426950408889634
HEADS = 20
GROUP = 4
CHUNKS = HEADS // GROUP
LANES = GROUP * 128
BF16 = jnp.bfloat16
F32 = jnp.float32
HIGHEST = lax.Precision.HIGHEST


def iota(shape, dim):
    return lax.broadcasted_iota(jnp.int32, shape, dim)


def onehot(cond, dtype=BF16):
    return jnp.where(cond, 1.0, 0.0).astype(dtype)


def dot(a, b, ca, cb, precision=None):
    return lax.dot_general(
        a, b, (((ca,), (cb,)), ((), ())), preferred_element_type=F32, precision=precision
    )


def squash(t):
    t = t.astype(F32)
    size = jnp.log2(1.0 + jnp.abs(t)) / 3.0
    return jnp.where(t < 0, -size, size)


def hidden_before(first, offset):
    n = iota((256, 1), 0)
    dy, dx = n // 16, n % 16
    cy = squash(jnp.where(dy >= 8, dy - 16, dy))
    cx = squash(jnp.where(dx >= 8, dx - 16, dx))
    return cy * first[0:1, :] + cx * first[1:2, :] + offset, cy, cx


def used_bins(rows):
    n = iota((rows, 256), 1)
    return (n // 16 != 8) & (n % 16 != 8)


def three_parts(x):
    a = x.astype(BF16)
    rest = x - a.astype(F32)
    b = rest.astype(BF16)
    c = (rest - b.astype(F32)).astype(BF16)
    return jnp.concatenate([a, b, c], axis=0)


def gather_matrix(shift, lat_shift):
    west = shift <= 4
    m = shift if west else 8 - shift
    w, n = iota((128, 128), 0), iota((128, 128), 1)
    lat = (lat_shift + w // 8) % 16
    col = w % 8 + (shift if west else -m)
    own = (n // 8 == lat) & (n % 8 == col)
    w, q = iota((128, 16 * m), 0), iota((128, 16 * m), 1)
    lat = (lat_shift + w // 8) % 16
    borrowed = (q % 16 == lat) & (w % 8 == (8 - shift if west else 0) + q // 16)
    return onehot(own), onehot(borrowed)


def place_matrix(shift, lat_shift):
    west = shift <= 4
    m = shift if west else 8 - shift
    n, w = iota((128, 128), 0), iota((128, 128), 1)
    lat = (lat_shift + w // 8) % 16
    col = w % 8 + (shift if west else -m)
    own = (n // 8 == lat) & (n % 8 == col)
    n, q = iota((128, 16 * m), 0), iota((128, 16 * m), 1)
    back = (n // 8 == q % 16) & (n % 8 == (0 if west else shift) + q // 16)
    return onehot(own), onehot(back)


def main_kernel(
    shift,
    q_ref,
    k_ref,
    v_ref,
    d_ref,
    land_ref,
    shifts_ref,
    first_ref,
    offset_ref,
    second_ref,
    keybias_ref,
    grads_ref,
    sums_ref,
    seconds_ref,
    held,
    packed,
    packed_back,
    bias,
    expand,
    rows,
    land_rows,
    gather_own,
    gather_far,
    table_part,
    core_part,
    z_part,
    xy_part,
    total,
    load_sem,
    in_send,
    in_recv,
    back_send,
    back_recv,
    second_sem,
    core_sem,
    z_send,
    z_recv,
    xy_send,
    xy_recv,
    all_send,
    all_recv,
):
    west = shift <= 4
    m = shift if west else 8 - shift
    y = lax.axis_index("dp")
    sp = lax.axis_index("space")
    t = lax.axis_index("tensor")
    core, z, x_lo = sp % 2, (sp // 2) % 8, sp // 16
    x = t * 2 + x_lo
    west_id = {"space": (sp + 31) % 32}
    east_id = {"space": (sp + 1) % 32}
    core_id = {"space": sp + 1 - 2 * core}
    z_ids = [{"space": x_lo * 16 + ((z + k) % 8) * 2 + core} for k in range(1, 8)]
    xy_ids = []
    for k in range(1, 16):
        xx, yy = (x + k // 4) % 4, (y + k % 4) % 4
        xy_ids.append({"dp": yy, "space": (xx % 2) * 16 + z * 2 + core, "tensor": xx // 2})
    tensor_id = {"tensor": 1 - t}

    loads = [
        pltpu.make_async_copy(ref, held.at[a, pl.ds(0, 16)], load_sem.at[a])
        for a, ref in enumerate((q_ref, k_ref, v_ref, d_ref))
    ]
    for copy in loads:
        copy.start()

    barrier = pltpu.get_barrier_semaphore()
    for to in [west_id, east_id] + z_ids + xy_ids:
        pl.semaphore_signal(barrier, inc=1, device_id=to, device_id_type=MESH)

    lat_shift = shifts_ref[0]
    own, far = gather_matrix(shift, lat_shift)
    gather_own[...] = own
    gather_far[...] = far
    out_id, back_id = (west_id, east_id) if west else (east_id, west_id)

    def in_copy(c):
        lanes = pl.ds(pl.multiple_of(c * LANES, LANES), LANES)
        return pltpu.make_async_remote_copy(
            src_ref=packed.at[:, :, :, lanes],
            dst_ref=held.at[:, pl.ds(16, 2 * m), :, lanes],
            send_sem=in_send.at[c],
            recv_sem=in_recv.at[c],
            device_id=out_id,
            device_id_type=MESH,
        )

    def back_copy(c):
        lanes = pl.ds(pl.multiple_of(c * LANES, LANES), LANES)
        return pltpu.make_async_remote_copy(
            src_ref=packed_back.at[:, :, :, lanes],
            dst_ref=grads_ref.at[:, pl.ds(16, 2 * m), :, lanes],
            send_sem=back_send.at[c],
            recv_sem=back_recv.at[c],
            device_id=back_id,
            device_id_type=MESH,
        )

    for copy in loads:
        copy.wait()
    r, n = iota((16 * m, 128), 0), iota((16 * m, 128), 1)
    pack = onehot((n // 8 == r % 16) & (n % 8 == (0 if west else shift) + r // 16))
    pl.semaphore_wait(barrier, 24)

    @pl.loop(0, CHUNKS)
    def _(c):
        lanes = pl.ds(pl.multiple_of(c * LANES, LANES), LANES)
        for a in range(4):
            part = held[a, 0:16, :, lanes].reshape(128, LANES)
            packed[a, :, :, lanes] = dot(pack, part, 1, 0).astype(BF16).reshape(2 * m, 8, LANES)
        in_copy(c).start()

    seconds_ref[t] = second_ref[...]
    second_copy = pltpu.make_async_remote_copy(
        src_ref=second_ref,
        dst_ref=seconds_ref.at[t],
        send_sem=second_sem.at[0],
        recv_sem=second_sem.at[1],
        device_id=tensor_id,
        device_id_type=MESH,
    )
    second_copy.start()

    pre, _, _ = hidden_before(first_ref[...], offset_ref[...])
    logits = dot(second_ref[...], jnp.maximum(pre, 0.0), 1, 1, HIGHEST)
    table = jnp.where(used_bins(HEADS), 16.0 * jax.nn.sigmoid(logits), 0.0)
    table = three_parts(jnp.concatenate([table, jnp.zeros((4, 256), F32)], axis=0))
    b, l = iota((256, 128), 0), iota((256, 128), 1)
    for cj in range(8):
        here = (b == (l // 8) * 16 + (l % 8 - cj + 16) % 16) | (b == 8) | (b == 24)
        sel = onehot(here)
        expand[:, cj * 128 : (cj + 1) * 128] = sel
        wide = dot(table, sel, 1, 0)
        wide = wide[0:24] + wide[24:48] + wide[48:72]
        rows[pl.ds(cj, HEADS, stride=8), :] = wide[0:HEADS]

    g, l = iota((256, 128), 0), iota((256, 128), 1)
    first_col = (sp if west else sp + 31) * 8 + shift
    columns = onehot(g == (first_col + l) % 256)
    land_cols = dot(land_ref[...].astype(F32).astype(BF16), columns, 1, 0).astype(BF16)
    j, l = iota((64, 128), 0), iota((64, 128), 1)
    halves = []
    for blk in range(2):
        jj, lat = iota((64, 16), 0), iota((64, 16), 1)
        pick = onehot(lat == (lat_shift + jj // 8 + 8 * blk) % 16)
        spread = dot(pick, land_cols, 1, 0)
        halves.append(jnp.sum(jnp.where(l == j % 8, spread, 0.0), axis=1, keepdims=True))
    is_land = jnp.where(l < 64, halves[0], halves[1])
    apart = (l >= 64) & ((j // 8 < 8 - lat_shift) != ((l % 64) // 8 < 8 - lat_shift))
    masked = jnp.where(apart, MASKED * LOG2E, 0.0)

    @pl.loop(0, HEADS)
    def _(h):
        one = rows[pl.ds(pl.multiple_of(h * 8, 8), 8), :]
        lane = iota((8, 128), 1)
        low, high = keybias_ref[0, h] * LOG2E, keybias_ref[1, h] * LOG2E
        for rj in range(8):
            left = pltpu.roll(one, 8 * rj, 1) if rj else one
            right = pltpu.roll(one, 8 * rj + 64, 1)
            at = slice(8 * rj, 8 * rj + 8)
            key = jnp.where(is_land[at] > 0.5, high, low) + masked[at]
            bias[h, at, :] = jnp.where(lane < 64, left, right) * LOG2E + key

    scale = 128.0 ** -0.5

    @pl.loop(0, CHUNKS)
    def _(c):
        in_copy(c).wait_recv()
        lane = iota((64, 128), 1)
        front = lane < 64
        base = pl.multiple_of(c * LANES, LANES)
        whole = pl.ds(base, LANES)

        def merged(a):
            mine = dot(gather_own[...], held[a, 0:16, :, whole].reshape(128, LANES), 1, 0)
            theirs = dot(
                gather_far[...], held[a, 16 : 16 + 2 * m, :, whole].reshape(16 * m, LANES), 1, 0
            )
            return (mine + theirs).astype(BF16)

        def paired(x):
            return jnp.where(front, x[0:64], x[64:128])

        def split(x):
            x = x.astype(F32)
            return jnp.concatenate(
                [jnp.where(front, x, 0.0), jnp.where(front, 0.0, x)], axis=0
            ).astype(BF16)

        qw, kw, vw, dw = [merged(a) for a in range(4)]
        cut = [slice(128 * i, 128 * i + 128) for i in range(GROUP)]
        scores = [paired(dot(kw[:, s], qw[:, s], 1, 1)) for s in cut]
        dprobs = [paired(dot(vw[:, s], dw[:, s], 1, 1)) for s in cut]
        probs, dscores = [], []
        for i in range(GROUP):
            sc = scores[i] * (scale * LOG2E) + bias[c * GROUP + i]
            e = jnp.exp2(sc - jnp.max(sc, axis=0, keepdims=True))
            p = e * (1.0 / jnp.sum(e, axis=0, keepdims=True))
            pd = p * dprobs[i]
            probs.append(p)
            dscores.append(pd - p * jnp.sum(pd, axis=0, keepdims=True))
        lane8 = iota((8, 128), 1)
        for i in range(GROUP):
            ds = dscores[i]
            acc = jnp.zeros((8, 128), F32)
            land_acc = jnp.zeros((8, 128), F32)
            for rj in range(8):
                at = slice(8 * rj, 8 * rj + 8)
                part = ds[at]
                land_acc += part * is_land[at]
                both = jnp.where(lane8 < 64, part + pltpu.roll(part, 64, 1), 0.0)
                acc += pltpu.roll(both, 128 - 8 * rj, 1) if rj else both
            at = pl.ds(pl.multiple_of((c * GROUP + i) * 8, 8), 8)
            rows[at, :] = acc
            land_rows[at, :] = land_acc
        gq, gk, gv = [], [], []
        for i in range(GROUP):
            s = cut[i]
            pl_low, ds_low = split(probs[i]), split(dscores[i])
            gv.append(dot(pl_low, dw[:, s], 1, 0))
            gk.append(dot(ds_low, qw[:, s], 1, 0) * scale)
            gq.append(dot(ds_low, kw[:, s], 0, 0) * scale)
        for a, parts in enumerate((gq, gk, gv)):
            value = jnp.concatenate(parts, axis=1).astype(BF16)
            grads_ref[a, 0:16, :, whole] = value.reshape(16, 8, LANES)
            packed_back[a, :, :, whole] = (
                dot(gather_far[...], value, 0, 0).astype(BF16).reshape(2 * m, 8, LANES)
            )
        back_copy(c).start()

    pad = jnp.zeros((4, 1024), F32)
    flat = jnp.concatenate([rows[pl.ds(cj, HEADS, stride=8), :] for cj in range(8)], axis=1)
    land_flat = jnp.concatenate(
        [land_rows[pl.ds(cj, HEADS, stride=8), :] for cj in range(8)], axis=1
    )
    stacked = three_parts(jnp.concatenate([flat, pad, land_flat, pad], axis=0))
    binned = dot(stacked, expand[...], 1, 1)
    binned = binned[0:48] + binned[48:96] + binned[96:144]
    binned = jnp.where(iota((24, 256), 1) == 24, binned[24:48], binned[0:24])
    for i in range(6):
        table_part[i] = binned[(i // 2) * 8 : (i // 2) * 8 + 8, (i % 2) * 128 : (i % 2) * 128 + 128]
    table_part[6:8] = jnp.zeros((2, 8, 128), F32)

    copy = pltpu.make_async_remote_copy(
        src_ref=table_part,
        dst_ref=core_part,
        send_sem=core_sem.at[0],
        recv_sem=core_sem.at[1],
        device_id=core_id,
        device_id_type=MESH,
    )
    copy.start()
    copy.wait()
    table_part[...] = table_part[...] + core_part[...]

    copies = []
    for k in range(1, 8):
        copies.append(
            pltpu.make_async_remote_copy(
                src_ref=table_part.at[(z + k) % 8],
                dst_ref=z_part.at[z],
                send_sem=z_send.at[k - 1],
                recv_sem=z_recv.at[k - 1],
                device_id=z_ids[k - 1],
                device_id_type=MESH,
            )
        )
    for copy in copies:
        copy.start()
    z_part[z] = table_part[z]
    for copy in copies:
        copy.wait()
    mine = z_part[0]
    for i in range(1, 8):
        mine = mine + z_part[i]

    xy_part[x * 4 + y] = mine
    copies = []
    for k in range(1, 16):
        copies.append(
            pltpu.make_async_remote_copy(
                src_ref=xy_part.at[x * 4 + y],
                dst_ref=xy_part.at[x * 4 + y],
                send_sem=xy_send.at[k - 1],
                recv_sem=xy_recv.at[k - 1],
                device_id=xy_ids[k - 1],
                device_id_type=MESH,
            )
        )
    for copy in copies:
        copy.start()
    for copy in copies:
        copy.wait()
    for half in range(2):
        mine = xy_part[half * 8]
        for i in range(1, 8):
            mine = mine + xy_part[half * 8 + i]
        total[z, half] = mine

    copies = []
    for k in range(1, 8):
        copies.append(
            pltpu.make_async_remote_copy(
                src_ref=total.at[z],
                dst_ref=total.at[z],
                send_sem=all_send.at[k - 1],
                recv_sem=all_recv.at[k - 1],
                device_id=z_ids[k - 1],
                device_id_type=MESH,
            )
        )
    for copy in copies:
        copy.start()
    for copy in copies:
        copy.wait()
    sums_ref[...] = total[...]

    second_copy.wait()

    @pl.loop(0, CHUNKS)
    def _(c):
        in_copy(c).wait_send()
        back_copy(c).wait()


def last_kernel(
    shift,
    grads_ref,
    sums_ref,
    seconds_ref,
    shifts_ref,
    first_ref,
    offset_ref,
    gq_ref,
    gk_ref,
    gv_ref,
    gfirst_ref,
    goffset_ref,
    gsecond_ref,
    gkey_ref,
):
    m = min(shift, 8 - shift)
    t = lax.axis_index("tensor")
    own, back = place_matrix(shift, shifts_ref[0])
    for a, out in enumerate((gq_ref, gk_ref, gv_ref)):
        for c in range(CHUNKS):
            lanes = slice(c * LANES, c * LANES + LANES)
            mine = dot(own, grads_ref[a, 0:16, :, lanes].reshape(128, LANES), 1, 0)
            theirs = dot(back, grads_ref[a, 16 : 16 + 2 * m, :, lanes].reshape(16 * m, LANES), 1, 0)
            out[:, :, lanes] = (mine + theirs).astype(BF16).reshape(16, 8, LANES)

    pre, cy, cx = hidden_before(first_ref[...], offset_ref[...])
    hidden = jnp.maximum(pre, 0.0)

    def bins(half):
        strips = [
            jnp.concatenate([sums_ref[2 * i, half], sums_ref[2 * i + 1, half]], axis=1)
            for i in range(3)
        ]
        return jnp.concatenate(strips, axis=0)

    def pulled(half):
        logits = dot(seconds_ref[half], hidden, 1, 1, HIGHEST)
        p = jax.nn.sigmoid(logits)
        return jnp.where(used_bins(HEADS), bins(half)[0:HEADS] * (16.0 * p * (1.0 - p)), 0.0)

    low, high = pulled(0), pulled(1)
    mine = jnp.where(t == 0, low, high)
    gsecond_ref[...] = dot(mine, hidden, 1, 0, HIGHEST)
    ghidden = dot(low, seconds_ref[0], 0, 0, HIGHEST) + dot(high, seconds_ref[1], 0, 0, HIGHEST)
    ghidden = jnp.where(pre > 0.0, ghidden, 0.0)
    gfirst_ref[0:1, :] = jnp.sum(cy * ghidden, axis=0, keepdims=True)
    gfirst_ref[1:2, :] = jnp.sum(cx * ghidden, axis=0, keepdims=True)
    goffset_ref[...] = jnp.sum(ghidden, axis=0, keepdims=True)
    r, n = iota((8, 256), 0), iota((8, 256), 1)
    pick = jnp.where(n == 24, jnp.where(r == 0, -1.0, 1.0), jnp.where((n == 8) & (r == 0), 1.0, 0.0))
    keys = dot(pick, jnp.where(t == 0, bins(0), bins(1)), 1, 1, HIGHEST)
    gkey_ref[...] = keys[0:2, 0:HEADS]


def on_device(q, k, v, d, land, shifts, first, offset, second, keybias):
    shape = q.shape
    fields = [a.reshape(16, 8, HEADS * 128) for a in (q, k, v, d)]
    offset = offset.reshape(1, 512)
    second = second.T
    vmem = pl.BlockSpec(memory_space=pltpu.VMEM)
    smem = pl.BlockSpec(memory_space=pltpu.SMEM)
    hbm = pl.BlockSpec(memory_space=pl.ANY)
    dma = pltpu.SemaphoreType.DMA

    def branch(shift):
        m = min(shift, 8 - shift)

        def run(q, k, v, d, land, shifts, first, offset, second, keybias):
            grads, sums, seconds = pl.pallas_call(
                functools.partial(main_kernel, shift),
                out_shape=(
                    jax.ShapeDtypeStruct((3, 16 + 2 * m, 8, HEADS * 128), BF16),
                    jax.ShapeDtypeStruct((8, 2, 8, 128), F32),
                    jax.ShapeDtypeStruct((2, HEADS, 512), F32),
                ),
                in_specs=[hbm] * 4 + [vmem, smem, vmem, vmem, vmem, smem],
                out_specs=(vmem, vmem, vmem),
                scratch_shapes=[
                    pltpu.VMEM((4, 16 + 2 * m, 8, HEADS * 128), BF16),
                    pltpu.VMEM((4, 2 * m, 8, HEADS * 128), BF16),
                    pltpu.VMEM((3, 2 * m, 8, HEADS * 128), BF16),
                    pltpu.VMEM((HEADS, 64, 128), F32),
                    pltpu.VMEM((256, 1024), BF16),
                    pltpu.VMEM((HEADS * 8, 128), F32),
                    pltpu.VMEM((HEADS * 8, 128), F32),
                    pltpu.VMEM((128, 128), BF16),
                    pltpu.VMEM((128, 16 * m), BF16),
                    pltpu.VMEM((8, 8, 128), F32),
                    pltpu.VMEM((8, 8, 128), F32),
                    pltpu.VMEM((8, 8, 128), F32),
                    pltpu.VMEM((16, 8, 128), F32),
                    pltpu.VMEM((8, 2, 8, 128), F32),
                    dma((4,)),
                    dma((CHUNKS,)),
                    dma((CHUNKS,)),
                    dma((CHUNKS,)),
                    dma((CHUNKS,)),
                    dma((2,)),
                    dma((2,)),
                    dma((7,)),
                    dma((7,)),
                    dma((15,)),
                    dma((15,)),
                    dma((7,)),
                    dma((7,)),
                ],
                compiler_params=pltpu.CompilerParams(
                    collective_id=shift, has_side_effects=True, vmem_limit_bytes=48 * 2**20
                ),
                name="exchange_and_grads",
            )(q, k, v, d, land, shifts, first, offset, second, keybias)
            return pl.pallas_call(
                functools.partial(last_kernel, shift),
                out_shape=(jax.ShapeDtypeStruct((16, 8, HEADS * 128), BF16),) * 3
                + (
                    jax.ShapeDtypeStruct((2, 512), F32),
                    jax.ShapeDtypeStruct((1, 512), F32),
                    jax.ShapeDtypeStruct((HEADS, 512), F32),
                    jax.ShapeDtypeStruct((2, HEADS), F32),
                ),
                in_specs=[vmem, vmem, vmem, smem, vmem, vmem],
                out_specs=(vmem,) * 7,
                compiler_params=pltpu.CompilerParams(vmem_limit_bytes=48 * 2**20),
                name="place_and_reduce",
            )(grads, sums, seconds, shifts, first, offset)

        return run

    out = lax.switch(
        jnp.clip(shifts[1] - 1, 0, 6),
        [branch(s) for s in range(1, 8)],
        *fields, land, shifts, first, offset, second, keybias,
    )
    gq, gk, gv, gfirst, goffset, gsecond, gkey = out
    return (
        gq.reshape(shape),
        gk.reshape(shape),
        gv.reshape(shape),
        gfirst,
        goffset.reshape(512),
        gsecond.T,
        gkey,
    )


def solution(mesh):
    field = P("dp", None, "space", "tensor")
    second = P(None, "tensor")
    return jax.shard_map(
        on_device,
        mesh=mesh,
        in_specs=(field,) * 4 + (P(), P(), P(), P(), second, second),
        out_specs=(field,) * 3 + (P(), P(), second, second),
        check_vma=False,
    )
```

```python
import jax
import jax.numpy as jnp
from jax import lax
from jax.experimental import pallas as pl
from jax.experimental.pallas import tpu as pltpu
from jax.sharding import PartitionSpec as P

MESH = pl.DeviceIdType.MESH
MASKED = -1000000000.0
LOG2E = 1.4426950408889634
HEADS = 20
HALF = HEADS // 2
PAIR = 2
CHUNKS = HALF // PAIR
LANES = PAIR * 128
EAST = HALF * 128
BF16 = jnp.bfloat16
F32 = jnp.float32
HIGHEST = lax.Precision.HIGHEST


def iota(shape, dim):
    return lax.broadcasted_iota(jnp.int32, shape, dim)


def onehot(cond):
    return jnp.where(cond, 1.0, 0.0).astype(BF16)


def dot(a, b, ca, cb, precision=None):
    return lax.dot_general(
        a, b, (((ca,), (cb,)), ((), ())), preferred_element_type=F32, precision=precision
    )


def squash(t):
    t = t.astype(F32)
    size = jnp.log2(1.0 + jnp.abs(t)) / 3.0
    return jnp.where(t < 0, -size, size)


def hidden_before(first, offset):
    n = iota((256, 1), 0)
    dy, dx = n // 16, n % 16
    cy = squash(jnp.where(dy >= 8, dy - 16, dy))
    cx = squash(jnp.where(dx >= 8, dx - 16, dx))
    return cy * first[0:1, :] + cx * first[1:2, :] + offset, cy, cx


def used_bins(rows):
    n = iota((rows, 256), 1)
    return (n // 16 != 8) & (n % 16 != 8)


def three_parts(x):
    a = x.astype(BF16)
    rest = x - a.astype(F32)
    b = rest.astype(BF16)
    c = (rest - b.astype(F32)).astype(BF16)
    return jnp.concatenate([a, b, c], axis=0)


def main_kernel(
    q_ref,
    k_ref,
    v_ref,
    d_ref,
    land_hbm,
    shifts_hbm,
    first_hbm,
    offset_hbm,
    second_hbm,
    keybias_hbm,
    out_ref,
    sums_ref,
    seconds_ref,
    layer_ref,
    held,
    far,
    arrived,
    bias,
    expand,
    rows,
    land_rows,
    is_land,
    gather,
    place,
    table_part,
    near_part,
    z_part,
    land_ref,
    second_ref,
    shifts_ref,
    keybias_ref,
    load_sem,
    small_sem,
    in_send,
    in_recv,
    back_send,
    back_recv,
    second_sem,
    near_send,
    near_recv,
    z_send,
    z_recv,
    xy_send,
    xy_recv,
):
    y = lax.axis_index("dp")
    sp = lax.axis_index("space")
    t = lax.axis_index("tensor")
    core, z, x_lo = sp % 2, (sp // 2) % 8, sp // 16
    x = t * 2 + x_lo
    west_id = {"space": (sp + 31) % 32}
    east_id = {"space": (sp + 1) % 32}
    slow_id = {"space": (sp + 31 + 2 * core) % 32}
    near = []
    for k in range(1, 16):
        xx, yy, cc = (x_lo + k // 8) % 2, (y + (k // 2) % 4) % 4, (core + k) % 2
        near.append((xx * 4 + yy, {"dp": yy, "space": xx * 16 + z * 2 + cc}))
    z_ids = [{"space": x_lo * 16 + ((z + k) % 8) * 2 + core} for k in range(1, 8)]
    xy_ids = []
    for k in range(1, 16):
        xx, yy = (x + k // 4) % 4, (y + k % 4) % 4
        xy_ids.append({"dp": yy, "space": (xx % 2) * 16 + z * 2 + core, "tensor": xx // 2})
    other_ids = []
    for k in range(8):
        xx, yy = (x_lo + k // 4) % 2, (y + k % 4) % 4
        other_ids.append({"dp": yy, "space": xx * 16 + z * 2 + core, "tensor": 1 - t})
    tensor_id = {"tensor": 1 - t}

    barrier = pltpu.get_barrier_semaphore()
    for to in [slow_id] + [i for _, i in near] + z_ids + other_ids:
        pl.semaphore_signal(barrier, inc=1, device_id=to, device_id_type=MESH)

    fields = (q_ref, k_ref, v_ref, d_ref)
    small = [
        pltpu.make_async_copy(a, b, small_sem.at[i])
        for i, (a, b) in enumerate(
            (
                (shifts_hbm, shifts_ref),
                (land_hbm, land_ref),
                (first_hbm, layer_ref.at[pl.ds(0, 2)]),
                (offset_hbm, layer_ref.at[pl.ds(2, 1)]),
                (second_hbm, second_ref),
                (keybias_hbm, keybias_ref),
            )
        )
    ]
    for copy in small:
        copy.start()

    def lanes_of(side, c):
        return pl.ds(pl.multiple_of(side * EAST + c * LANES, LANES), LANES)

    def in_copy(side, a, c):
        lanes = lanes_of(side, c)
        return pltpu.make_async_remote_copy(
            src_ref=fields[a].at[:, :, lanes],
            dst_ref=held.at[a, pl.ds(16 - 16 * side, 16), :, lanes],
            send_sem=in_send.at[side, a, c],
            recv_sem=in_recv.at[side, a, c],
            device_id=east_id if side else west_id,
            device_id_type=MESH,
        )

    def back_copy(side, c):
        lanes = lanes_of(side, c)
        return pltpu.make_async_remote_copy(
            src_ref=far.at[:, :, :, lanes],
            dst_ref=arrived.at[:, :, :, lanes],
            send_sem=back_send.at[side, c],
            recv_sem=back_recv.at[side, c],
            device_id=west_id if side else east_id,
            device_id_type=MESH,
        )

    second_copy = pltpu.make_async_remote_copy(
        src_ref=second_hbm,
        dst_ref=seconds_ref.at[t],
        send_sem=second_sem.at[0],
        recv_sem=second_sem.at[1],
        device_id=tensor_id,
        device_id_type=MESH,
    )
    loads = []
    for a in range(4):
        for side in range(2):
            lanes = pl.ds(side * EAST, EAST)
            loads.append(
                pltpu.make_async_copy(
                    fields[a].at[:, :, lanes],
                    held.at[a, pl.ds(16 * side, 16), :, lanes],
                    load_sem.at[a, side],
                )
            )

    pl.semaphore_wait(barrier, 31)

    @pl.loop(0, CHUNKS)
    def _(c):
        for a in range(4):
            for side in range(2):
                in_copy(side, a, c).start()

    second_copy.start()
    for copy in loads:
        copy.start()
    for copy in small:
        copy.wait()
    seconds_ref[t] = second_ref[...]

    lat_shift, lon_shift = shifts_ref[0], shifts_ref[1]
    w, n = iota((128, 256), 0), iota((128, 256), 1)
    same = (lat_shift + w // 8) % 16 == (n // 8) % 16
    gather[...] = onehot(same & (w % 8 + lon_shift == n % 8 + 8 * (n // 128)))
    n, w = iota((256, 128), 0), iota((256, 128), 1)
    same = (lat_shift + w // 8) % 16 == (n // 8) % 16
    place[...] = onehot(same & (w % 8 + lon_shift == n % 8 + 8 * (n // 128)))

    pre, _, _ = hidden_before(layer_ref[0:2, :], layer_ref[2:3, :])
    logits = dot(second_ref[...], jnp.maximum(pre, 0.0), 1, 1, HIGHEST)
    table = jnp.where(used_bins(HEADS), 16.0 * jax.nn.sigmoid(logits), 0.0)
    table = three_parts(jnp.concatenate([table, jnp.zeros((4, 256), F32)], axis=0))
    b, l = iota((256, 128), 0), iota((256, 128), 1)
    for cj in range(8):
        here = (b == (l // 8) * 16 + (l % 8 - cj + 16) % 16) | (b == 8) | (b == 24)
        sel = onehot(here)
        expand[:, cj * 128 : (cj + 1) * 128] = sel
        wide = dot(table, sel, 1, 0)
        wide = wide[0:24] + wide[24:48] + wide[48:72]
        rows[pl.ds(cj, HEADS, stride=8), :] = wide[0:HEADS]

    j, l = iota((64, 128), 0), iota((64, 128), 1)
    land = land_ref[...].astype(F32).astype(BF16)
    for side in range(2):
        g, l = iota((256, 128), 0), iota((256, 128), 1)
        first_col = (sp + 31 * side) * 8 + lon_shift
        land_cols = dot(land, onehot(g == (first_col + l) % 256), 1, 0).astype(BF16)
        j, l = iota((64, 128), 0), iota((64, 128), 1)
        halves = []
        for blk in range(2):
            jj, lat = iota((64, 16), 0), iota((64, 16), 1)
            pick = onehot(lat == (lat_shift + jj // 8 + 8 * blk) % 16)
            spread = dot(pick, land_cols, 1, 0)
            halves.append(jnp.sum(jnp.where(l == j % 8, spread, 0.0), axis=1, keepdims=True))
        is_land[side] = jnp.where(l < 64, halves[0], halves[1])
    apart = (l >= 64) & ((j // 8 < 8 - lat_shift) != ((l % 64) // 8 < 8 - lat_shift))
    masked = jnp.where(apart, MASKED * LOG2E, 0.0)

    for side in range(2):

        @pl.loop(side * HALF, side * HALF + HALF)
        def _(h):
            one = rows[pl.ds(pl.multiple_of(h * 8, 8), 8), :]
            lane = iota((8, 128), 1)
            low, high = keybias_ref[0, h] * LOG2E, keybias_ref[1, h] * LOG2E
            for rj in range(8):
                left = pltpu.roll(one, 8 * rj, 1) if rj else one
                right = pltpu.roll(one, 8 * rj + 64, 1)
                at = slice(8 * rj, 8 * rj + 8)
                key = jnp.where(is_land[side, at] > 0.5, high, low) + masked[at]
                bias[h, at, :] = jnp.where(lane < 64, left, right) * LOG2E + key

    for copy in loads:
        copy.wait()
    scale = 128.0 ** -0.5

    @pl.loop(0, CHUNKS)
    def _(c):
        front = iota((64, 128), 1) < 64

        def paired(x):
            return jnp.where(front, x[0:64], x[64:128])

        def split(x):
            return jnp.concatenate(
                [jnp.where(front, x, 0.0), jnp.where(front, 0.0, x)], axis=0
            ).astype(BF16)

        for side in range(2):
            for a in range(4):
                in_copy(side, a, c).wait_recv()
        merged = []
        for side in range(2):
            lanes = lanes_of(side, c)
            for a in range(4):
                both = held[a, :, :, lanes].reshape(256, LANES)
                merged.append(dot(gather[...], both, 1, 0).astype(BF16))
        work = []
        for side in range(2):
            for i in range(PAIR):
                s = slice(128 * i, 128 * i + 128)
                work.append((side, side * HALF + c * PAIR + i, [merged[side * 4 + a][:, s] for a in range(4)]))
        scores = [paired(dot(f[1], f[0], 1, 1)) for _, _, f in work]
        dprobs = [paired(dot(f[2], f[3], 1, 1)) for _, _, f in work]
        probs, dscores = [], []
        for (side, h, _), score, dprob in zip(work, scores, dprobs):
            sc = score * (scale * LOG2E) + bias[h]
            e = jnp.exp2(sc - jnp.max(sc, axis=0, keepdims=True))
            p = e * (1.0 / jnp.sum(e, axis=0, keepdims=True))
            pd = p * dprob
            probs.append(p)
            dscores.append(pd - p * jnp.sum(pd, axis=0, keepdims=True))
        lane8 = iota((8, 128), 1)
        for (side, h, _), ds in zip(work, dscores):
            acc = jnp.zeros((8, 128), F32)
            land_acc = jnp.zeros((8, 128), F32)
            for rj in range(8):
                at = slice(8 * rj, 8 * rj + 8)
                part = ds[at]
                land_acc += part * is_land[side, at]
                both = jnp.where(lane8 < 64, part + pltpu.roll(part, 64, 1), 0.0)
                acc += pltpu.roll(both, 128 - 8 * rj, 1) if rj else both
            at = pl.ds(pl.multiple_of(h * 8, 8), 8)
            rows[at, :] = acc
            land_rows[at, :] = land_acc
        grads = []
        for (side, h, f), p, ds in zip(work, probs, dscores):
            p_low, ds_low = split(p), split(ds)
            grads.append(
                (
                    dot(ds_low, f[1], 0, 0) * scale,
                    dot(ds_low, f[0], 1, 0) * scale,
                    dot(p_low, f[3], 1, 0),
                )
            )
        for side in range(2):
            lanes = lanes_of(side, c)
            for a in range(3):
                value = jnp.concatenate(
                    [grads[side * PAIR + i][a] for i in range(PAIR)], axis=1
                ).astype(BF16)
                placed = dot(place[...], value, 1, 0).astype(BF16)
                here = placed[128 * side : 128 * side + 128]
                there = placed[128 - 128 * side : 256 - 128 * side]
                out_ref[a, :, :, lanes] = here.reshape(16, 8, LANES)
                far[a, :, :, lanes] = there.reshape(16, 8, LANES)
            back_copy(side, c).start()

    pad = jnp.zeros((4, 1024), F32)
    flat = jnp.concatenate([rows[pl.ds(cj, HEADS, stride=8), :] for cj in range(8)], axis=1)
    land_flat = jnp.concatenate(
        [land_rows[pl.ds(cj, HEADS, stride=8), :] for cj in range(8)], axis=1
    )
    stacked = three_parts(jnp.concatenate([flat, pad, land_flat, pad], axis=0))
    binned = dot(stacked, expand[...], 1, 1)
    binned = binned[0:48] + binned[48:96] + binned[96:144]
    binned = jnp.where(iota((24, 256), 1) == 24, binned[24:48], binned[0:24])
    for i in range(6):
        table_part[i] = binned[(i // 2) * 8 : (i // 2) * 8 + 8, (i % 2) * 128 : (i % 2) * 128 + 128]
    table_part[6:8] = jnp.zeros((2, 8, 128), F32)

    def exchange(pieces):
        return [
            pltpu.make_async_remote_copy(
                src_ref=src,
                dst_ref=dst,
                send_sem=send.at[i],
                recv_sem=recv.at[i],
                device_id=to,
                device_id_type=MESH,
            )
            for i, (src, dst, send, recv, to) in enumerate(pieces)
        ]

    def add_arrived(c):
        for side in range(2):
            lanes = lanes_of(side, c)
            back_copy(side, c).wait_recv()
            for a in range(3):
                out_ref[a, :, :, lanes] = out_ref[a, :, :, lanes] + arrived[a, :, :, lanes]

    slot = x_lo * 4 + y
    copies = exchange(
        [(table_part.at[i], near_part.at[slot * 2 + core], near_send, near_recv, to) for i, to in near]
    )
    for copy in copies:
        copy.start()
    near_part[slot * 2 + core] = table_part[slot]
    for copy in copies:
        copy.wait()
    mine = near_part[0]
    for i in range(1, 16):
        mine = mine + near_part[i]

    z_part[z] = mine
    copies = exchange([(z_part.at[z], z_part.at[z], z_send, z_recv, to) for to in z_ids])
    for copy in copies:
        copy.start()

    @pl.loop(0, 2)
    def _(c):
        add_arrived(c)

    for copy in copies:
        copy.wait()
    mine = z_part[0]
    for i in range(1, 8):
        mine = mine + z_part[i]

    sums_ref[x * 4 + y] = mine
    here = sums_ref.at[x * 4 + y]
    copies = exchange([(here, here, xy_send, xy_recv, to) for to in xy_ids])
    for copy in copies:
        copy.start()

    @pl.loop(2, CHUNKS)
    def _(c):
        add_arrived(c)

    second_copy.wait()

    @pl.loop(0, CHUNKS)
    def _(c):
        for side in range(2):
            for a in range(4):
                in_copy(side, a, c).wait_send()
            back_copy(side, c).wait_send()

    for copy in copies:
        copy.wait()


def last_kernel(
    grads_ref,
    sums_hbm,
    seconds_hbm,
    layer_hbm,
    gq_ref,
    gk_ref,
    gv_ref,
    gfirst_ref,
    goffset_ref,
    gsecond_ref,
    gkey_ref,
    sums_ref,
    seconds_ref,
    layer_ref,
    held,
    sem,
):
    small = [
        pltpu.make_async_copy(a, b, sem.at[3 + i])
        for i, (a, b) in enumerate(
            ((layer_hbm, layer_ref), (seconds_hbm, seconds_ref), (sums_hbm, sums_ref))
        )
    ]
    for copy in small:
        copy.start()
    outs = (gq_ref, gk_ref, gv_ref)
    loads = [pltpu.make_async_copy(grads_ref.at[a], held.at[a], sem.at[6 + a]) for a in range(3)]
    copies = [pltpu.make_async_copy(held.at[a], outs[a], sem.at[a]) for a in range(3)]
    for copy in loads:
        copy.start()
    for copy in small:
        copy.wait()
    for load, copy in zip(loads, copies):
        load.wait()
        copy.start()
    t = lax.axis_index("tensor")
    pre, cy, cx = hidden_before(layer_ref[0:2, :], layer_ref[2:3, :])
    hidden = jnp.maximum(pre, 0.0)

    def bins(half):
        strips = [
            jnp.concatenate([sums_ref[half * 8 + 2 * i], sums_ref[half * 8 + 2 * i + 1]], axis=1)
            for i in range(3)
        ]
        return jnp.concatenate(strips, axis=0)

    def pulled(half):
        logits = dot(seconds_ref[half], hidden, 1, 1, HIGHEST)
        p = jax.nn.sigmoid(logits)
        return jnp.where(used_bins(HEADS), bins(half)[0:HEADS] * (16.0 * p * (1.0 - p)), 0.0)

    low, high = pulled(0), pulled(1)
    mine = jnp.where(t == 0, low, high)
    gsecond_ref[...] = dot(mine, hidden, 1, 0, HIGHEST)
    ghidden = dot(low, seconds_ref[0], 0, 0, HIGHEST) + dot(high, seconds_ref[1], 0, 0, HIGHEST)
    ghidden = jnp.where(pre > 0.0, ghidden, 0.0)
    gfirst_ref[0:1, :] = jnp.sum(cy * ghidden, axis=0, keepdims=True)
    gfirst_ref[1:2, :] = jnp.sum(cx * ghidden, axis=0, keepdims=True)
    goffset_ref[...] = jnp.sum(ghidden, axis=0, keepdims=True)
    r, n = iota((8, 256), 0), iota((8, 256), 1)
    pick = jnp.where(n == 24, jnp.where(r == 0, -1.0, 1.0), jnp.where((n == 8) & (r == 0), 1.0, 0.0))
    keys = dot(pick, jnp.where(t == 0, bins(0), bins(1)), 1, 1, HIGHEST)
    gkey_ref[...] = keys[0:2, 0:HEADS]
    for copy in copies:
        copy.wait()


def on_device(q, k, v, d, land, shifts, first, offset, second, keybias):
    shape = q.shape
    field = (16, 8, HEADS * 128)
    fields = [a.reshape(field) for a in (q, k, v, d)]
    vmem = pl.BlockSpec(memory_space=pltpu.VMEM)
    hbm = pl.BlockSpec(memory_space=pltpu.HBM)
    dma = pltpu.SemaphoreType.DMA
    vec = pltpu.VMEM
    outs = pl.pallas_call(
        main_kernel,
        out_shape=(
            jax.ShapeDtypeStruct((3,) + field, BF16),
            jax.ShapeDtypeStruct((16, 8, 128), F32),
            jax.ShapeDtypeStruct((2, HEADS, 512), F32),
            jax.ShapeDtypeStruct((3, 512), F32),
        ),
        in_specs=[hbm] * 10,
        out_specs=(vmem,) * 4,
        scratch_shapes=[
            vec((4, 32, 8, HEADS * 128), BF16),
            vec((3,) + field, BF16),
            vec((3,) + field, BF16),
            vec((HEADS, 64, 128), F32),
            vec((256, 1024), BF16),
            vec((HEADS * 8, 128), F32),
            vec((HEADS * 8, 128), F32),
            vec((2, 64, 128), F32),
            vec((128, 256), BF16),
            vec((256, 128), BF16),
            vec((8, 8, 128), F32),
            vec((16, 8, 128), F32),
            vec((8, 8, 128), F32),
            vec((16, 256), jnp.int32),
            vec((HEADS, 512), F32),
            pltpu.SMEM((2,), jnp.int32),
            pltpu.SMEM((2, HEADS), F32),
            dma((4, 2)),
            dma((6,)),
            dma((2, 4, CHUNKS)),
            dma((2, 4, CHUNKS)),
            dma((2, CHUNKS)),
            dma((2, CHUNKS)),
            dma((2,)),
            dma((15,)),
            dma((15,)),
            dma((7,)),
            dma((7,)),
            dma((15,)),
            dma((15,)),
        ],
        compiler_params=pltpu.CompilerParams(
            collective_id=0, has_side_effects=True, vmem_limit_bytes=60 * 2**20
        ),
        name="exchange_and_grads",
    )(*fields, land, shifts, first, offset.reshape(1, 512), second.T, keybias)
    gq, gk, gv, gfirst, goffset, gsecond, gkey = pl.pallas_call(
        last_kernel,
        out_shape=(jax.ShapeDtypeStruct(field, BF16),) * 3
        + (
            jax.ShapeDtypeStruct((2, 512), F32),
            jax.ShapeDtypeStruct((1, 512), F32),
            jax.ShapeDtypeStruct((HEADS, 512), F32),
            jax.ShapeDtypeStruct((2, HEADS), F32),
        ),
        in_specs=[hbm] * 4,
        out_specs=(hbm,) * 3 + (vmem,) * 4,
        scratch_shapes=[
            vec((16, 8, 128), F32),
            vec((2, HEADS, 512), F32),
            vec((3, 512), F32),
            vec((3,) + field, BF16),
            dma((9,)),
        ],
        compiler_params=pltpu.CompilerParams(vmem_limit_bytes=60 * 2**20),
        name="write_and_reduce",
    )(*outs)
    return (
        gq.reshape(shape),
        gk.reshape(shape),
        gv.reshape(shape),
        gfirst,
        goffset.reshape(512),
        gsecond.T,
        gkey,
    )


def solution(mesh):
    field = P("dp", None, "space", "tensor")
    second = P(None, "tensor")
    return jax.shard_map(
        on_device,
        mesh=mesh,
        in_specs=(field,) * 4 + (P(), P(), P(), P(), second, second),
        out_specs=(field,) * 3 + (P(), P(), second, second),
        check_vma=False,
    )
```

```python
import jax
import jax.numpy as jnp
from jax import lax
from jax.experimental import pallas as pl
from jax.experimental.pallas import tpu as pltpu
from jax.sharding import PartitionSpec as P

MESH = pl.DeviceIdType.MESH
MASKED = -1000000000.0
LOG2E = 1.4426950408889634
HEADS = 20
GROUP = 4
CHUNKS = HEADS // GROUP
LANES = GROUP * 128
ROOM = 9
SIDE = ROOM * 16
BOTH = 2 * SIDE
BF16 = jnp.bfloat16
F32 = jnp.float32
HIGHEST = lax.Precision.HIGHEST


def iota(shape, dim):
    return lax.broadcasted_iota(jnp.int32, shape, dim)


def onehot(cond):
    return jnp.where(cond, 1.0, 0.0).astype(BF16)


def dot(a, b, ca, cb, precision=None):
    return lax.dot_general(
        a, b, (((ca,), (cb,)), ((), ())), preferred_element_type=F32, precision=precision
    )


def squash(t):
    t = t.astype(F32)
    size = jnp.log2(1.0 + jnp.abs(t)) / 3.0
    return jnp.where(t < 0, -size, size)


def hidden_before(first, offset):
    n = iota((256, 1), 0)
    dy, dx = n // 16, n % 16
    cy = squash(jnp.where(dy >= 8, dy - 16, dy))
    cx = squash(jnp.where(dx >= 8, dx - 16, dx))
    return cy * first[0:1, :] + cx * first[1:2, :] + offset, cy, cx


def used_bins(rows):
    n = iota((rows, 256), 1)
    return (n // 16 != 8) & (n % 16 != 8)


def three_parts(x):
    a = x.astype(BF16)
    rest = x - a.astype(F32)
    b = rest.astype(BF16)
    c = (rest - b.astype(F32)).astype(BF16)
    return jnp.concatenate([a, b, c], axis=0)


def west_heads(shift):
    return jnp.where(shift <= 2, 4, jnp.where(shift >= 6, 0, 6 - shift))


def block_of(head, column, shift, west):
    return jnp.where(
        head < west, head * shift + column, ROOM + (head - west) * (8 - shift) + column - shift
    )


def patch_code(head, n, shift, west):
    lat, column = n // 8, n % 8
    leaves = (head < west) == (column < shift)
    return jnp.where(leaves, block_of(head, column, shift, west) * 16 + lat, -1)


def window_place(head, w, shift, lat_shift, west):
    lat = (lat_shift + w // 8) % 16
    column = w % 8 + shift
    over = column >= 8
    return over == (head < west), jnp.where(over, column - 8, column), lat


def main_kernel(
    q_ref,
    k_ref,
    v_ref,
    d_ref,
    land_hbm,
    shifts_hbm,
    first_hbm,
    offset_hbm,
    second_hbm,
    keybias_hbm,
    out_ref,
    sums_ref,
    seconds_ref,
    layer_ref,
    held,
    own,
    packed,
    lent,
    window,
    far,
    arrived,
    bias,
    expand,
    rows,
    land_rows,
    is_land,
    pack_in,
    pack_back,
    merge,
    place,
    table_part,
    near_part,
    z_part,
    land_ref,
    second_ref,
    shifts_ref,
    keybias_ref,
    load_sem,
    small_sem,
    in_send,
    in_recv,
    back_send,
    back_recv,
    second_sem,
    near_send,
    near_recv,
    z_send,
    z_recv,
    xy_send,
    xy_recv,
):
    y = lax.axis_index("dp")
    sp = lax.axis_index("space")
    t = lax.axis_index("tensor")
    core, z, x_lo = sp % 2, (sp // 2) % 8, sp // 16
    x = t * 2 + x_lo
    west_id = {"space": (sp + 31) % 32}
    east_id = {"space": (sp + 1) % 32}
    slow_id = {"space": (sp + 31 + 2 * core) % 32}
    near = []
    for k in range(1, 16):
        xx, yy, cc = (x_lo + k // 8) % 2, (y + (k // 2) % 4) % 4, (core + k) % 2
        near.append((xx * 4 + yy, {"dp": yy, "space": xx * 16 + z * 2 + cc}))
    z_ids = [{"space": x_lo * 16 + ((z + k) % 8) * 2 + core} for k in range(1, 8)]
    xy_ids = []
    for k in range(1, 16):
        xx, yy = (x + k // 4) % 4, (y + k % 4) % 4
        xy_ids.append({"dp": yy, "space": (xx % 2) * 16 + z * 2 + core, "tensor": xx // 2})
    other_ids = []
    for k in range(8):
        xx, yy = (x_lo + k // 4) % 2, (y + k % 4) % 4
        other_ids.append({"dp": yy, "space": xx * 16 + z * 2 + core, "tensor": 1 - t})
    tensor_id = {"tensor": 1 - t}

    fields = (q_ref, k_ref, v_ref, d_ref)
    small = [
        pltpu.make_async_copy(a, b, small_sem.at[i])
        for i, (a, b) in enumerate(
            (
                (shifts_hbm, shifts_ref),
                (land_hbm, land_ref),
                (first_hbm, layer_ref.at[pl.ds(0, 2)]),
                (offset_hbm, layer_ref.at[pl.ds(2, 1)]),
                (second_hbm, second_ref),
                (keybias_hbm, keybias_ref),
            )
        )
    ]
    loads = [pltpu.make_async_copy(ref, held.at[a], load_sem.at[a]) for a, ref in enumerate(fields)]
    small[0].start()
    for copy in loads:
        copy.start()
    for copy in small[1:]:
        copy.start()

    barrier = pltpu.get_barrier_semaphore()
    for to in [slow_id] + [i for _, i in near] + z_ids + other_ids:
        pl.semaphore_signal(barrier, inc=1, device_id=to, device_id_type=MESH)

    def side_rows(side):
        return pl.ds(side * SIDE, SIDE)

    def in_copy(side, c):
        return pltpu.make_async_remote_copy(
            src_ref=packed.at[c, side_rows(side)],
            dst_ref=lent.at[c, side_rows(side)],
            send_sem=in_send.at[side, c],
            recv_sem=in_recv.at[side, c],
            device_id=east_id if side else west_id,
            device_id_type=MESH,
        )

    def back_copy(side, c):
        return pltpu.make_async_remote_copy(
            src_ref=far.at[c, side_rows(side)],
            dst_ref=arrived.at[c, side_rows(side)],
            send_sem=back_send.at[side, c],
            recv_sem=back_recv.at[side, c],
            device_id=west_id if side else east_id,
            device_id_type=MESH,
        )

    second_copy = pltpu.make_async_remote_copy(
        src_ref=second_hbm,
        dst_ref=seconds_ref.at[t],
        send_sem=second_sem.at[0],
        recv_sem=second_sem.at[1],
        device_id=tensor_id,
        device_id_type=MESH,
    )

    small[0].wait()
    lat_shift, shift = shifts_ref[0], shifts_ref[1]
    west = west_heads(shift)
    e = iota((1, GROUP * 128), 1)
    code = patch_code(e // 128, e % 128, shift, west)
    pack_in[...] = onehot(iota((BOTH, GROUP * 128), 0) == code)

    def pack(c):
        for i in range(GROUP):
            lanes = pl.ds(pl.multiple_of(c * LANES, LANES) + 128 * i, 128)
            for a in range(4):
                own[c, 128 * i : 128 * i + 128, 128 * a : 128 * a + 128] = held[
                    a, :, :, lanes
                ].reshape(128, 128)
        packed[c] = dot(pack_in[...], own[c], 1, 0).astype(BF16)

    for copy in loads:
        copy.wait()
    pack(0)
    pl.semaphore_wait(barrier, 31)
    for side in range(2):
        in_copy(side, 0).start()

    @pl.loop(1, CHUNKS)
    def _(c):
        pack(c)
        for side in range(2):
            in_copy(side, c).start()

    second_copy.start()
    for copy in small[1:]:
        copy.wait()
    seconds_ref[t] = second_ref[...]

    borrowed, column, lat = window_place(e // 128, e % 128, shift, lat_shift, west)
    code = jnp.where(borrowed, block_of(e // 128, column, shift, west) * 16 + lat, -1)
    pack_back[...] = onehot(iota((BOTH, GROUP * 128), 0) == code)
    for i in range(GROUP):
        n, target = iota((128, 1), 0), iota((128, 128 + BOTH), 1)
        borrowed, column, lat = window_place(i, n, shift, lat_shift, west)
        code = block_of(i, column, shift, west) * 16 + lat
        merge[i] = onehot(target == jnp.where(borrowed, 128 + code, lat * 8 + column))
        code = patch_code(i, n, shift, west)
        row = (n // 8 + 16 - lat_shift) % 16
        here = row * 8 + (n % 8 + 8 - shift) % 8
        place[i] = onehot(target == jnp.where(code >= 0, 128 + code, here))

    pre, _, _ = hidden_before(layer_ref[0:2, :], layer_ref[2:3, :])
    logits = dot(second_ref[...], jnp.maximum(pre, 0.0), 1, 1, HIGHEST)
    table = jnp.where(used_bins(HEADS), 16.0 * jax.nn.sigmoid(logits), 0.0)
    table = three_parts(jnp.concatenate([table, jnp.zeros((4, 256), F32)], axis=0))
    b, l = iota((256, 128), 0), iota((256, 128), 1)
    for cj in range(8):
        here = (b == (l // 8) * 16 + (l % 8 - cj + 16) % 16) | (b == 8) | (b == 24)
        sel = onehot(here)
        expand[:, cj * 128 : (cj + 1) * 128] = sel
        wide = dot(table, sel, 1, 0)
        wide = wide[0:24] + wide[24:48] + wide[48:72]
        rows[pl.ds(cj, HEADS, stride=8), :] = wide[0:HEADS]

    land = land_ref[...].astype(F32).astype(BF16)
    j, l = iota((64, 128), 0), iota((64, 128), 1)
    lands = []
    for side in range(2):
        g, cols = iota((256, 128), 0), iota((256, 128), 1)
        first_col = (sp + 31 * side) * 8 + shift
        land_cols = dot(land, onehot(g == (first_col + cols) % 256), 1, 0).astype(BF16)
        halves = []
        for blk in range(2):
            jj, lat = iota((64, 16), 0), iota((64, 16), 1)
            pick = onehot(lat == (lat_shift + jj // 8 + 8 * blk) % 16)
            spread = dot(pick, land_cols, 1, 0)
            halves.append(jnp.sum(jnp.where(l == j % 8, spread, 0.0), axis=1, keepdims=True))
        lands.append(jnp.where(l < 64, halves[0], halves[1]))
    for i in range(GROUP):
        is_land[i] = jnp.where(i < west, lands[0], lands[1])
    apart = (l >= 64) & ((j // 8 < 8 - lat_shift) != ((l % 64) // 8 < 8 - lat_shift))
    masked = jnp.where(apart, MASKED * LOG2E, 0.0)

    @pl.loop(0, CHUNKS)
    def _(c):
        lane = iota((8, 128), 1)
        for i in range(GROUP):
            h = c * GROUP + i
            one = rows[pl.ds(pl.multiple_of(h * 8, 8), 8), :]
            low, high = keybias_ref[0, h] * LOG2E, keybias_ref[1, h] * LOG2E
            for rj in range(8):
                left = pltpu.roll(one, 8 * rj, 1) if rj else one
                right = pltpu.roll(one, 8 * rj + 64, 1)
                at = slice(8 * rj, 8 * rj + 8)
                key = jnp.where(is_land[i, at] > 0.5, high, low) + masked[at]
                bias[h, at, :] = jnp.where(lane < 64, left, right) * LOG2E + key

    scale = 128.0 ** -0.5

    @pl.loop(0, CHUNKS)
    def _(c):
        front = iota((64, 128), 1) < 64

        def paired(x):
            return jnp.where(front, x[0:64], x[64:128])

        def split(x):
            return jnp.concatenate(
                [jnp.where(front, x, 0.0), jnp.where(front, 0.0, x)], axis=0
            ).astype(BF16)

        for side in range(2):
            in_copy(side, c).wait_recv()
        theirs = lent[c]
        merged = []
        for i in range(GROUP):
            both = jnp.concatenate([own[c, 128 * i : 128 * i + 128, :], theirs], axis=0)
            whole = dot(merge[i], both, 1, 0).astype(BF16)
            merged.append([whole[:, 128 * a : 128 * a + 128] for a in range(4)])
        scores = [paired(dot(f[1], f[0], 1, 1)) for f in merged]
        dprobs = [paired(dot(f[2], f[3], 1, 1)) for f in merged]
        probs, dscores = [], []
        for i in range(GROUP):
            sc = scores[i] * (scale * LOG2E) + bias[c * GROUP + i]
            e = jnp.exp2(sc - jnp.max(sc, axis=0, keepdims=True))
            p = e * (1.0 / jnp.sum(e, axis=0, keepdims=True))
            pd = p * dprobs[i]
            probs.append(p)
            dscores.append(pd - p * jnp.sum(pd, axis=0, keepdims=True))
        lane8 = iota((8, 128), 1)
        for i in range(GROUP):
            acc = jnp.zeros((8, 128), F32)
            land_acc = jnp.zeros((8, 128), F32)
            for rj in range(8):
                at = slice(8 * rj, 8 * rj + 8)
                part = dscores[i][at]
                land_acc += part * is_land[i, at]
                both = jnp.where(lane8 < 64, part + pltpu.roll(part, 64, 1), 0.0)
                acc += pltpu.roll(both, 128 - 8 * rj, 1) if rj else both
            at = pl.ds(pl.multiple_of((c * GROUP + i) * 8, 8), 8)
            rows[at, :] = acc
            land_rows[at, :] = land_acc
        for i in range(GROUP):
            f, at = merged[i], slice(128 * i, 128 * i + 128)
            p_low, ds_low = split(probs[i]), split(dscores[i])
            window[c, at, 0:128] = (dot(ds_low, f[1], 0, 0) * scale).astype(BF16)
            window[c, at, 128:256] = (dot(ds_low, f[0], 1, 0) * scale).astype(BF16)
            window[c, at, 256:384] = dot(p_low, f[3], 1, 0).astype(BF16)
        far[c] = dot(pack_back[...], window[c], 1, 0).astype(BF16)
        for side in range(2):
            back_copy(side, c).start()

    pad = jnp.zeros((4, 1024), F32)
    flat = jnp.concatenate([rows[pl.ds(cj, HEADS, stride=8), :] for cj in range(8)], axis=1)
    land_flat = jnp.concatenate(
        [land_rows[pl.ds(cj, HEADS, stride=8), :] for cj in range(8)], axis=1
    )
    stacked = three_parts(jnp.concatenate([flat, pad, land_flat, pad], axis=0))
    binned = dot(stacked, expand[...], 1, 1)
    binned = binned[0:48] + binned[48:96] + binned[96:144]
    binned = jnp.where(iota((24, 256), 1) == 24, binned[24:48], binned[0:24])
    for i in range(6):
        table_part[i] = binned[(i // 2) * 8 : (i // 2) * 8 + 8, (i % 2) * 128 : (i % 2) * 128 + 128]
    table_part[6:8] = jnp.zeros((2, 8, 128), F32)

    def exchange(pieces):
        return [
            pltpu.make_async_remote_copy(
                src_ref=src,
                dst_ref=dst,
                send_sem=send.at[i],
                recv_sem=recv.at[i],
                device_id=to,
                device_id_type=MESH,
            )
            for i, (src, dst, send, recv, to) in enumerate(pieces)
        ]

    def finish(c):
        for side in range(2):
            back_copy(side, c).wait_recv()
        theirs = arrived[c]
        for i in range(GROUP):
            lanes = pl.ds(pl.multiple_of(c * LANES, LANES) + 128 * i, 128)
            both = jnp.concatenate([window[c, 128 * i : 128 * i + 128, :], theirs], axis=0)
            whole = dot(place[i], both, 1, 0).astype(BF16)
            for a in range(3):
                out_ref[a, :, :, lanes] = whole[:, 128 * a : 128 * a + 128].reshape(16, 8, 128)

    slot = x_lo * 4 + y
    copies = exchange(
        [(table_part.at[i], near_part.at[slot * 2 + core], near_send, near_recv, to) for i, to in near]
    )
    for copy in copies:
        copy.start()
    near_part[slot * 2 + core] = table_part[slot]
    for copy in copies:
        copy.wait()
    mine = near_part[0]
    for i in range(1, 16):
        mine = mine + near_part[i]

    z_part[z] = mine
    copies = exchange([(z_part.at[z], z_part.at[z], z_send, z_recv, to) for to in z_ids])
    for copy in copies:
        copy.start()

    @pl.loop(0, 2)
    def _(c):
        finish(c)

    for copy in copies:
        copy.wait()
    mine = z_part[0]
    for i in range(1, 8):
        mine = mine + z_part[i]

    sums_ref[x * 4 + y] = mine
    here = sums_ref.at[x * 4 + y]
    copies = exchange([(here, here, xy_send, xy_recv, to) for to in xy_ids])
    for copy in copies:
        copy.start()

    @pl.loop(2, CHUNKS)
    def _(c):
        finish(c)

    second_copy.wait()

    @pl.loop(0, CHUNKS)
    def _(c):
        for side in range(2):
            in_copy(side, c).wait_send()
            back_copy(side, c).wait_send()

    for copy in copies:
        copy.wait()


def last_kernel(
    grads_ref,
    sums_hbm,
    seconds_hbm,
    layer_hbm,
    gq_ref,
    gk_ref,
    gv_ref,
    gfirst_ref,
    goffset_ref,
    gsecond_ref,
    gkey_ref,
    sums_ref,
    seconds_ref,
    layer_ref,
    held,
    sem,
):
    small = [
        pltpu.make_async_copy(a, b, sem.at[3 + i])
        for i, (a, b) in enumerate(
            ((layer_hbm, layer_ref), (seconds_hbm, seconds_ref), (sums_hbm, sums_ref))
        )
    ]
    for copy in small:
        copy.start()
    outs = (gq_ref, gk_ref, gv_ref)
    loads = [pltpu.make_async_copy(grads_ref.at[a], held.at[a], sem.at[6 + a]) for a in range(3)]
    copies = [pltpu.make_async_copy(held.at[a], outs[a], sem.at[a]) for a in range(3)]
    for copy in loads:
        copy.start()
    for copy in small:
        copy.wait()
    for load, copy in zip(loads, copies):
        load.wait()
        copy.start()
    t = lax.axis_index("tensor")
    pre, cy, cx = hidden_before(layer_ref[0:2, :], layer_ref[2:3, :])
    hidden = jnp.maximum(pre, 0.0)

    def bins(half):
        strips = [
            jnp.concatenate([sums_ref[half * 8 + 2 * i], sums_ref[half * 8 + 2 * i + 1]], axis=1)
            for i in range(3)
        ]
        return jnp.concatenate(strips, axis=0)

    def pulled(half):
        logits = dot(seconds_ref[half], hidden, 1, 1, HIGHEST)
        p = jax.nn.sigmoid(logits)
        return jnp.where(used_bins(HEADS), bins(half)[0:HEADS] * (16.0 * p * (1.0 - p)), 0.0)

    low, high = pulled(0), pulled(1)
    mine = jnp.where(t == 0, low, high)
    gsecond_ref[...] = dot(mine, hidden, 1, 0, HIGHEST)
    ghidden = dot(low, seconds_ref[0], 0, 0, HIGHEST) + dot(high, seconds_ref[1], 0, 0, HIGHEST)
    ghidden = jnp.where(pre > 0.0, ghidden, 0.0)
    gfirst_ref[0:1, :] = jnp.sum(cy * ghidden, axis=0, keepdims=True)
    gfirst_ref[1:2, :] = jnp.sum(cx * ghidden, axis=0, keepdims=True)
    goffset_ref[...] = jnp.sum(ghidden, axis=0, keepdims=True)
    r, n = iota((8, 256), 0), iota((8, 256), 1)
    pick = jnp.where(n == 24, jnp.where(r == 0, -1.0, 1.0), jnp.where((n == 8) & (r == 0), 1.0, 0.0))
    keys = dot(pick, jnp.where(t == 0, bins(0), bins(1)), 1, 1, HIGHEST)
    gkey_ref[...] = keys[0:2, 0:HEADS]
    for copy in copies:
        copy.wait()


def on_device(q, k, v, d, land, shifts, first, offset, second, keybias):
    shape = q.shape
    field = (16, 8, HEADS * 128)
    fields = [a.reshape(field) for a in (q, k, v, d)]
    vmem = pl.BlockSpec(memory_space=pltpu.VMEM)
    hbm = pl.BlockSpec(memory_space=pltpu.HBM)
    dma = pltpu.SemaphoreType.DMA
    vec = pltpu.VMEM
    outs = pl.pallas_call(
        main_kernel,
        out_shape=(
            jax.ShapeDtypeStruct((3,) + field, BF16),
            jax.ShapeDtypeStruct((16, 8, 128), F32),
            jax.ShapeDtypeStruct((2, HEADS, 512), F32),
            jax.ShapeDtypeStruct((3, 512), F32),
        ),
        in_specs=[hbm] * 10,
        out_specs=(vmem,) * 4,
        scratch_shapes=[
            vec((4,) + field, BF16),
            vec((CHUNKS, GROUP * 128, 512), BF16),
            vec((CHUNKS, BOTH, 512), BF16),
            vec((CHUNKS, BOTH, 512), BF16),
            vec((CHUNKS, GROUP * 128, 384), BF16),
            vec((CHUNKS, BOTH, 384), BF16),
            vec((CHUNKS, BOTH, 384), BF16),
            vec((HEADS, 64, 128), F32),
            vec((256, 1024), BF16),
            vec((HEADS * 8, 128), F32),
            vec((HEADS * 8, 128), F32),
            vec((GROUP, 64, 128), F32),
            vec((BOTH, GROUP * 128), BF16),
            vec((BOTH, GROUP * 128), BF16),
            vec((GROUP, 128, 128 + BOTH), BF16),
            vec((GROUP, 128, 128 + BOTH), BF16),
            vec((8, 8, 128), F32),
            vec((16, 8, 128), F32),
            vec((8, 8, 128), F32),
            vec((16, 256), jnp.int32),
            vec((HEADS, 512), F32),
            pltpu.SMEM((2,), jnp.int32),
            pltpu.SMEM((2, HEADS), F32),
            dma((4,)),
            dma((6,)),
            dma((2, CHUNKS)),
            dma((2, CHUNKS)),
            dma((2, CHUNKS)),
            dma((2, CHUNKS)),
            dma((2,)),
            dma((15,)),
            dma((15,)),
            dma((7,)),
            dma((7,)),
            dma((15,)),
            dma((15,)),
        ],
        compiler_params=pltpu.CompilerParams(
            collective_id=0, has_side_effects=True, vmem_limit_bytes=60 * 2**20
        ),
        name="exchange_and_grads",
    )(*fields, land, shifts, first, offset.reshape(1, 512), second.T, keybias)
    gq, gk, gv, gfirst, goffset, gsecond, gkey = pl.pallas_call(
        last_kernel,
        out_shape=(jax.ShapeDtypeStruct(field, BF16),) * 3
        + (
            jax.ShapeDtypeStruct((2, 512), F32),
            jax.ShapeDtypeStruct((1, 512), F32),
            jax.ShapeDtypeStruct((HEADS, 512), F32),
            jax.ShapeDtypeStruct((2, HEADS), F32),
        ),
        in_specs=[hbm] * 4,
        out_specs=(hbm,) * 3 + (vmem,) * 4,
        scratch_shapes=[
            vec((16, 8, 128), F32),
            vec((2, HEADS, 512), F32),
            vec((3, 512), F32),
            vec((3,) + field, BF16),
            dma((9,)),
        ],
        compiler_params=pltpu.CompilerParams(vmem_limit_bytes=60 * 2**20),
        name="write_and_reduce",
    )(*outs)
    return (
        gq.reshape(shape),
        gk.reshape(shape),
        gv.reshape(shape),
        gfirst,
        goffset.reshape(512),
        gsecond.T,
        gkey,
    )


def solution(mesh):
    field = P("dp", None, "space", "tensor")
    second = P(None, "tensor")
    return jax.shard_map(
        on_device,
        mesh=mesh,
        in_specs=(field,) * 4 + (P(), P(), P(), P(), second, second),
        out_specs=(field,) * 3 + (P(), P(), second, second),
        check_vma=False,
    )
```

```python
import jax
import jax.numpy as jnp
from jax import lax
from jax.experimental import pallas as pl
from jax.experimental.pallas import tpu as pltpu
from jax.sharding import PartitionSpec as P

MESH = pl.DeviceIdType.MESH
MASKED = -1000000000.0
LOG2E = 1.4426950408889634
HEADS = 20
GROUP = 4
CHUNKS = HEADS // GROUP
LANES = GROUP * 128
ROOM = 9
SIDE = ROOM * 16
BOTH = 2 * SIDE
EARLY = 2
BF16 = jnp.bfloat16
F32 = jnp.float32
HIGHEST = lax.Precision.HIGHEST


def iota(shape, dim):
    return lax.broadcasted_iota(jnp.int32, shape, dim)


def onehot(cond):
    return jnp.where(cond, 1.0, 0.0).astype(BF16)


def dot(a, b, ca, cb, precision=None):
    return lax.dot_general(
        a, b, (((ca,), (cb,)), ((), ())), preferred_element_type=F32, precision=precision
    )


def squash(t):
    t = t.astype(F32)
    size = jnp.log2(1.0 + jnp.abs(t)) / 3.0
    return jnp.where(t < 0, -size, size)


def hidden_before(first, offset):
    n = iota((256, 1), 0)
    dy, dx = n // 16, n % 16
    cy = squash(jnp.where(dy >= 8, dy - 16, dy))
    cx = squash(jnp.where(dx >= 8, dx - 16, dx))
    return cy * first[0:1, :] + cx * first[1:2, :] + offset, cy, cx


def used_bins(rows):
    n = iota((rows, 256), 1)
    return (n // 16 != 8) & (n % 16 != 8)


def three_parts(x):
    a = x.astype(BF16)
    rest = x - a.astype(F32)
    b = rest.astype(BF16)
    c = (rest - b.astype(F32)).astype(BF16)
    return jnp.concatenate([a, b, c], axis=0)


def two_parts(x):
    a = x.astype(BF16)
    return a, (x - a.astype(F32)).astype(BF16)


def west_heads(shift):
    return jnp.where(shift <= 2, 4, jnp.where(shift >= 6, 0, 6 - shift))


def block_of(head, column, shift, west):
    return jnp.where(
        head < west, head * shift + column, ROOM + (head - west) * (8 - shift) + column - shift
    )


def patch_code(head, n, shift, west):
    lat, column = n // 8, n % 8
    leaves = (head < west) == (column < shift)
    return jnp.where(leaves, block_of(head, column, shift, west) * 16 + lat, -1)


def window_place(head, w, shift, lat_shift, west):
    lat = (lat_shift + w // 8) % 16
    column = w % 8 + shift
    over = column >= 8
    return over == (head < west), jnp.where(over, column - 8, column), lat


def main_kernel(
    q_ref,
    k_ref,
    v_ref,
    d_ref,
    land_hbm,
    shifts_hbm,
    first_hbm,
    offset_hbm,
    second_hbm,
    keybias_hbm,
    gq_hbm,
    gk_hbm,
    gv_hbm,
    gfirst_ref,
    goffset_ref,
    gsecond_ref,
    gkey_ref,
    out_ref,
    sums_ref,
    seconds_ref,
    layer_ref,
    hidden_ref,
    slope_ref,
    merged_ref,
    probs_ref,
    dscores_ref,
    held,
    own,
    packed,
    lent,
    window,
    far,
    arrived,
    bias,
    expand,
    rows,
    land_rows,
    is_land,
    pack_in,
    pack_back,
    merge,
    place,
    table_part,
    near_part,
    z_part,
    land_ref,
    second_ref,
    shifts_ref,
    keybias_ref,
    load_sem,
    small_sem,
    in_send,
    in_recv,
    back_send,
    back_recv,
    second_sem,
    near_send,
    near_recv,
    z_send,
    z_recv,
    xy_send,
    xy_recv,
    out_sem,
):
    y = lax.axis_index("dp")
    sp = lax.axis_index("space")
    t = lax.axis_index("tensor")
    core, z, x_lo = sp % 2, (sp // 2) % 8, sp // 16
    x = t * 2 + x_lo
    west_id = {"space": (sp + 31) % 32}
    east_id = {"space": (sp + 1) % 32}
    slow_id = {"space": (sp + 31 + 2 * core) % 32}
    near = []
    for k in sorted(range(1, 16), key=lambda k: -(k // 8 + 2 - abs((k // 2) % 4 - 2))):
        xx, yy, cc = (x_lo + k // 8) % 2, (y + (k // 2) % 4) % 4, (core + k) % 2
        near.append((xx * 4 + yy, {"dp": yy, "space": xx * 16 + z * 2 + cc}))
    z_ids = [{"space": x_lo * 16 + ((z + k) % 8) * 2 + core} for k in (4, 3, 5, 2, 6, 1, 7)]
    xy_ids = []
    for k in sorted(range(1, 16), key=lambda k: -(4 - abs(k // 4 - 2) - abs(k % 4 - 2))):
        xx, yy = (x + k // 4) % 4, (y + k % 4) % 4
        xy_ids.append({"dp": yy, "space": (xx % 2) * 16 + z * 2 + core, "tensor": xx // 2})
    other_ids = []
    for k in range(8):
        xx, yy = (x_lo + k // 4) % 2, (y + k % 4) % 4
        other_ids.append({"dp": yy, "space": xx * 16 + z * 2 + core, "tensor": 1 - t})
    tensor_id = {"tensor": 1 - t}

    greeted = z_ids + other_ids + [to for _, to in near] + [slow_id]
    barrier = pltpu.get_barrier_semaphore()
    for to in greeted:
        pl.semaphore_signal(barrier, inc=1, device_id=to, device_id_type=MESH)

    fields = (q_ref, k_ref, v_ref, d_ref)
    small = [
        pltpu.make_async_copy(a, b, small_sem.at[i])
        for i, (a, b) in enumerate(
            (
                (shifts_hbm, shifts_ref),
                (land_hbm, land_ref),
                (first_hbm, layer_ref.at[pl.ds(0, 2)]),
                (offset_hbm, layer_ref.at[pl.ds(2, 1)]),
                (second_hbm, second_ref),
                (keybias_hbm, keybias_ref),
            )
        )
    ]
    loads = [pltpu.make_async_copy(ref, held.at[a], load_sem.at[a]) for a, ref in enumerate(fields)]
    small[0].start()
    for copy in loads:
        copy.start()
    for copy in small[1:]:
        copy.start()

    def side_rows(side):
        return pl.ds(side * SIDE, SIDE)

    def in_copy(side, c):
        return pltpu.make_async_remote_copy(
            src_ref=packed.at[c, side_rows(side)],
            dst_ref=lent.at[c, side_rows(side)],
            send_sem=in_send.at[side, c],
            recv_sem=in_recv.at[side, c],
            device_id=east_id if side else west_id,
            device_id_type=MESH,
        )

    def back_copy(side, c):
        return pltpu.make_async_remote_copy(
            src_ref=far.at[c, side_rows(side)],
            dst_ref=arrived.at[c, side_rows(side)],
            send_sem=back_send.at[side, c],
            recv_sem=back_recv.at[side, c],
            device_id=west_id if side else east_id,
            device_id_type=MESH,
        )

    second_copy = pltpu.make_async_remote_copy(
        src_ref=second_hbm,
        dst_ref=seconds_ref.at[t],
        send_sem=second_sem.at[0],
        recv_sem=second_sem.at[1],
        device_id=tensor_id,
        device_id_type=MESH,
    )

    small[0].wait()
    lat_shift, shift = shifts_ref[0], shifts_ref[1]
    west = west_heads(shift)
    e = iota((1, GROUP * 128), 1)
    code = patch_code(e // 128, e % 128, shift, west)
    pack_in[...] = onehot(iota((BOTH, GROUP * 128), 0) == code)

    def pack(c):
        for i in range(GROUP):
            lanes = pl.ds(pl.multiple_of(c * LANES, LANES) + 128 * i, 128)
            for a in range(4):
                own[c, 128 * i : 128 * i + 128, 128 * a : 128 * a + 128] = held[
                    a, :, :, lanes
                ].reshape(128, 128)
        packed[c] = dot(pack_in[...], own[c], 1, 0).astype(BF16)

    for copy in loads:
        copy.wait()
    pack(0)
    pl.semaphore_wait(barrier, len(greeted))
    for side in range(2):
        in_copy(side, 0).start()

    @pl.loop(1, CHUNKS)
    def _(c):
        pack(c)
        for side in range(2):
            in_copy(side, c).start()

    second_copy.start()
    for copy in small[1:]:
        copy.wait()
    seconds_ref[t] = second_ref[...]

    borrowed, column, lat = window_place(e // 128, e % 128, shift, lat_shift, west)
    code = jnp.where(borrowed, block_of(e // 128, column, shift, west) * 16 + lat, -1)
    pack_back[...] = onehot(iota((BOTH, GROUP * 128), 0) == code)
    for i in range(GROUP):
        n, target = iota((128, 1), 0), iota((128, 128 + BOTH), 1)
        borrowed, column, lat = window_place(i, n, shift, lat_shift, west)
        code = block_of(i, column, shift, west) * 16 + lat
        merge[i] = onehot(target == jnp.where(borrowed, 128 + code, lat * 8 + column))
        code = patch_code(i, n, shift, west)
        row = (n // 8 + 16 - lat_shift) % 16
        here = row * 8 + (n % 8 + 8 - shift) % 8
        place[i] = onehot(target == jnp.where(code >= 0, 128 + code, here))

    pre, _, _ = hidden_before(layer_ref[0:2, :], layer_ref[2:3, :])
    logits = dot(second_ref[...], jnp.maximum(pre, 0.0), 1, 1, HIGHEST)
    table = jnp.where(used_bins(HEADS), 16.0 * jax.nn.sigmoid(logits), 0.0)
    table = three_parts(jnp.concatenate([table, jnp.zeros((4, 256), F32)], axis=0))
    b, l = iota((256, 128), 0), iota((256, 128), 1)
    for cj in range(8):
        here = (b == (l // 8) * 16 + (l % 8 - cj + 16) % 16) | (b == 8) | (b == 24)
        sel = onehot(here)
        expand[:, cj * 128 : (cj + 1) * 128] = sel
        wide = dot(table, sel, 1, 0)
        wide = wide[0:24] + wide[24:48] + wide[48:72]
        rows[pl.ds(cj, HEADS, stride=8), :] = wide[0:HEADS]

    land = land_ref[...].astype(F32).astype(BF16)
    j, l = iota((64, 128), 0), iota((64, 128), 1)
    lands = []
    for side in range(2):
        g, cols = iota((256, 128), 0), iota((256, 128), 1)
        first_col = (sp + 31 * side) * 8 + shift
        land_cols = dot(land, onehot(g == (first_col + cols) % 256), 1, 0).astype(BF16)
        halves = []
        for blk in range(2):
            jj, lat = iota((64, 16), 0), iota((64, 16), 1)
            pick = onehot(lat == (lat_shift + jj // 8 + 8 * blk) % 16)
            spread = dot(pick, land_cols, 1, 0)
            halves.append(jnp.sum(jnp.where(l == j % 8, spread, 0.0), axis=1, keepdims=True))
        lands.append(jnp.where(l < 64, halves[0], halves[1]))
    for i in range(GROUP):
        is_land[i] = jnp.where(i < west, lands[0], lands[1])
    apart = (l >= 64) & ((j // 8 < 8 - lat_shift) != ((l % 64) // 8 < 8 - lat_shift))
    masked = jnp.where(apart, MASKED * LOG2E, 0.0)

    @pl.loop(0, CHUNKS)
    def _(c):
        lane = iota((8, 128), 1)
        for i in range(GROUP):
            h = c * GROUP + i
            one = rows[pl.ds(pl.multiple_of(h * 8, 8), 8), :]
            low, high = keybias_ref[0, h] * LOG2E, keybias_ref[1, h] * LOG2E
            for rj in range(8):
                left = pltpu.roll(one, 8 * rj, 1) if rj else one
                right = pltpu.roll(one, 8 * rj + 64, 1)
                at = slice(8 * rj, 8 * rj + 8)
                key = jnp.where(is_land[i, at] > 0.5, high, low) + masked[at]
                bias[h, at, :] = jnp.where(lane < 64, left, right) * LOG2E + key

    scale = 128.0 ** -0.5

    front = iota((64, 128), 1) < 64
    lane8 = iota((8, 128), 1)

    def paired(x):
        return jnp.where(front, x[0:64], x[64:128])

    def split(x):
        return jnp.concatenate([jnp.where(front, x, 0.0), jnp.where(front, 0.0, x)], axis=0)

    def receive(c):
        for side in range(2):
            in_copy(side, c).wait_recv()

    def give_back(c):
        for side in range(2):
            back_copy(side, c).start()

    def attention(c):
        theirs = lent[c]
        merged = []
        for i in range(GROUP):
            both = jnp.concatenate([own[c, 128 * i : 128 * i + 128, :], theirs], axis=0)
            whole = dot(merge[i], both, 1, 0).astype(BF16)
            merged_ref[c % 2, i] = whole
            merged.append([whole[:, 128 * a : 128 * a + 128] for a in range(4)])
        scores = [paired(dot(f[1], f[0], 1, 1)) for f in merged]
        dprobs = [paired(dot(f[2], f[3], 1, 1)) for f in merged]
        for i in range(GROUP):
            h = c * GROUP + i
            sc = scores[i] * (scale * LOG2E) + bias[h]
            e = jnp.exp2(sc - jnp.max(sc, axis=0, keepdims=True))
            p = e * (1.0 / jnp.sum(e, axis=0, keepdims=True))
            pd = p * dprobs[i]
            ds = pd - p * jnp.sum(pd, axis=0, keepdims=True)
            probs_ref[c % 2, i] = split(p).astype(BF16)
            dscores_ref[c % 2, i] = split(ds).astype(BF16)
            acc = jnp.zeros((8, 128), F32)
            land_acc = jnp.zeros((8, 128), F32)
            for rj in range(8):
                at = slice(8 * rj, 8 * rj + 8)
                part = ds[at]
                land_acc += part * is_land[i, at]
                both = jnp.where(lane8 < 64, part + pltpu.roll(part, 64, 1), 0.0)
                acc += pltpu.roll(both, 128 - 8 * rj, 1) if rj else both
            at = pl.ds(pl.multiple_of(h * 8, 8), 8)
            rows[at, :] = acc
            land_rows[at, :] = land_acc

    def gradients(c):
        for i in range(GROUP):
            f, at = merged_ref[c % 2, i], slice(128 * i, 128 * i + 128)
            p_low, ds_low = probs_ref[c % 2, i], dscores_ref[c % 2, i]
            window[c, at, 0:128] = (dot(ds_low, f[:, 128:256], 0, 0) * scale).astype(BF16)
            window[c, at, 128:256] = (dot(ds_low, f[:, 0:128], 1, 0) * scale).astype(BF16)
            window[c, at, 256:384] = dot(p_low, f[:, 384:512], 1, 0).astype(BF16)
        far[c] = dot(pack_back[...], window[c], 1, 0).astype(BF16)

    receive(0)
    attention(0)

    @pl.loop(1, CHUNKS - 1)
    def _(c):
        receive(c)
        attention(c)
        gradients(c - 1)

        @pl.when(c <= EARLY)
        def _():
            give_back(c - 1)

    receive(CHUNKS - 1)
    attention(CHUNKS - 1)

    pad = jnp.zeros((4, 1024), F32)
    flat = jnp.concatenate([rows[pl.ds(cj, HEADS, stride=8), :] for cj in range(8)], axis=1)
    land_flat = jnp.concatenate(
        [land_rows[pl.ds(cj, HEADS, stride=8), :] for cj in range(8)], axis=1
    )
    stacked = three_parts(jnp.concatenate([flat, pad, land_flat, pad], axis=0))
    binned = dot(stacked, expand[...], 1, 1)
    binned = binned[0:48] + binned[48:96] + binned[96:144]
    binned = jnp.where(iota((24, 256), 1) == 24, binned[24:48], binned[0:24])
    for i in range(6):
        table_part[i] = binned[(i // 2) * 8 : (i // 2) * 8 + 8, (i % 2) * 128 : (i % 2) * 128 + 128]
    table_part[6:8] = jnp.zeros((2, 8, 128), F32)

    def exchange(pieces):
        return [
            pltpu.make_async_remote_copy(
                src_ref=src,
                dst_ref=dst,
                send_sem=send.at[i],
                recv_sem=recv.at[i],
                device_id=to,
                device_id_type=MESH,
            )
            for i, (src, dst, send, recv, to) in enumerate(pieces)
        ]

    def out_copies(c):
        lanes = pl.ds(pl.multiple_of(c * LANES, LANES), LANES)
        return [
            pltpu.make_async_copy(out_ref.at[a, :, :, lanes], out.at[:, :, lanes], out_sem.at[a, c])
            for a, out in enumerate((gq_hbm, gk_hbm, gv_hbm))
        ]

    def finish(c):
        for side in range(2):
            back_copy(side, c).wait_recv()
        theirs = arrived[c]
        for i in range(GROUP):
            lanes = pl.ds(pl.multiple_of(c * LANES, LANES) + 128 * i, 128)
            both = jnp.concatenate([window[c, 128 * i : 128 * i + 128, :], theirs], axis=0)
            whole = dot(place[i], both, 1, 0).astype(BF16)
            for a in range(3):
                out_ref[a, :, :, lanes] = whole[:, 128 * a : 128 * a + 128].reshape(16, 8, 128)
        for copy in out_copies(c):
            copy.start()

    slot = x_lo * 4 + y
    copies = exchange(
        [(table_part.at[i], near_part.at[slot * 2 + core], near_send, near_recv, to) for i, to in near]
    )
    for copy in copies:
        copy.start()
    near_part[slot * 2 + core] = table_part[slot]
    gradients(CHUNKS - 2)
    gradients(CHUNKS - 1)
    second_copy.wait()
    pre, cy, cx = hidden_before(layer_ref[0:2, :], layer_ref[2:3, :])
    hidden = jnp.maximum(pre, 0.0)
    hidden_ref[0], hidden_ref[1] = two_parts(hidden)
    sent = copies
    for copy in copies:
        copy.wait_recv()
    mine = near_part[0]
    for i in range(1, 16):
        mine = mine + near_part[i]

    z_part[z] = mine
    copies = exchange([(z_part.at[z], z_part.at[z], z_send, z_recv, to) for to in z_ids])
    for copy in copies:
        copy.start()

    for c in range(EARLY, CHUNKS):
        give_back(c)
    for half in range(2):
        p = jax.nn.sigmoid(dot(seconds_ref[half], hidden, 1, 1, HIGHEST))
        slope_ref[half] = jnp.where(used_bins(HEADS), 16.0 * p * (1.0 - p), 0.0)

    @pl.loop(0, 2)
    def _(c):
        finish(c)

    sent = sent + copies
    for copy in copies:
        copy.wait_recv()
    mine = z_part[0]
    for i in range(1, 8):
        mine = mine + z_part[i]

    sums_ref[x * 4 + y] = mine
    here = sums_ref.at[x * 4 + y]
    copies = exchange([(here, here, xy_send, xy_recv, to) for to in xy_ids])
    for copy in copies:
        copy.start()

    @pl.loop(2, CHUNKS)
    def _(c):
        finish(c)

    @pl.loop(0, CHUNKS)
    def _(c):
        for side in range(2):
            in_copy(side, c).wait_send()
            back_copy(side, c).wait_send()

    seconds = jnp.concatenate([seconds_ref[0], seconds_ref[1]], axis=0)
    seconds_high, seconds_low = two_parts(seconds)
    seconds_three = jnp.concatenate([seconds_high, seconds_high, seconds_low], axis=0)
    sent = sent + copies
    for copy in copies:
        copy.wait_recv()

    def bins(half):
        strips = [
            jnp.concatenate([sums_ref[half * 8 + 2 * i], sums_ref[half * 8 + 2 * i + 1]], axis=1)
            for i in range(3)
        ]
        return jnp.concatenate(strips, axis=0)

    pulled = [bins(half)[0:HEADS] * slope_ref[half] for half in range(2)]
    high, low = two_parts(jnp.where(t == 0, pulled[0], pulled[1]))
    gsecond = dot(jnp.concatenate([high, low], axis=0), hidden_ref[0], 1, 0)
    gsecond_ref[...] = (
        gsecond[0:HEADS] + gsecond[HEADS : 2 * HEADS] + dot(high, hidden_ref[1], 1, 0)
    )
    high, low = two_parts(jnp.concatenate(pulled, axis=0))
    ghidden = dot(jnp.concatenate([high, low, high], axis=0), seconds_three, 0, 0)
    ghidden = jnp.where(pre > 0.0, ghidden, 0.0)
    gfirst_ref[0:1, :] = jnp.sum(cy * ghidden, axis=0, keepdims=True)
    gfirst_ref[1:2, :] = jnp.sum(cx * ghidden, axis=0, keepdims=True)
    goffset_ref[...] = jnp.sum(ghidden, axis=0, keepdims=True)
    r, n = iota((8, 256), 0), iota((8, 256), 1)
    pick = jnp.where(n == 24, jnp.where(r == 0, -1.0, 1.0), jnp.where((n == 8) & (r == 0), 1.0, 0.0))
    keys = dot(pick, jnp.where(t == 0, bins(0), bins(1)), 1, 1, HIGHEST)
    gkey_ref[...] = keys[0:2, 0:HEADS]
    for copy in sent:
        copy.wait_send()

    @pl.loop(0, CHUNKS)
    def _(c):
        for copy in out_copies(c):
            copy.wait()


def last_kernel(*refs):
    n = len(refs) // 3
    given, placed, held, sem = refs[:n], refs[n : 2 * n], refs[2 * n : 3 * n], refs[3 * n]
    pieces = [(i, pl.ds(4 * part, 4)) for part in range(4) for i in range(3)]
    pieces += [(i, slice(None)) for i in range(3, n)]
    loads, copies = [], []
    for at, (i, part) in enumerate(pieces):
        here = held[i].at[part]
        loads.append(pltpu.make_async_copy(given[i].at[part], here, sem.at[0, at]))
        copies.append(pltpu.make_async_copy(here, placed[i].at[part], sem.at[1, at]))
    for load in loads:
        load.start()
    for load, copy in zip(loads, copies):
        load.wait()
        copy.start()
    for copy in copies:
        copy.wait()


def on_device(q, k, v, d, land, shifts, first, offset, second, keybias):
    shape = q.shape
    field = (16, 8, HEADS * 128)
    fields = [a.reshape(field) for a in (q, k, v, d)]
    vmem = pl.BlockSpec(memory_space=pltpu.VMEM)
    hbm = pl.BlockSpec(memory_space=pltpu.HBM)
    dma = pltpu.SemaphoreType.DMA
    vec = pltpu.VMEM
    results = (jax.ShapeDtypeStruct(field, BF16),) * 3 + (
        jax.ShapeDtypeStruct((2, 512), F32),
        jax.ShapeDtypeStruct((1, 512), F32),
        jax.ShapeDtypeStruct((HEADS, 512), F32),
        jax.ShapeDtypeStruct((2, HEADS), F32),
    )
    outs = pl.pallas_call(
        main_kernel,
        out_shape=results,
        in_specs=[hbm] * 10,
        out_specs=(hbm,) * 3 + (vmem,) * 4,
        scratch_shapes=[
            vec((3,) + field, BF16),
            vec((16, 8, 128), F32),
            vec((2, HEADS, 512), F32),
            vec((3, 512), F32),
            vec((2, 256, 512), BF16),
            vec((2, HEADS, 256), F32),
            vec((2, GROUP, 128, 512), BF16),
            vec((2, GROUP, 128, 128), BF16),
            vec((2, GROUP, 128, 128), BF16),
            vec((4,) + field, BF16),
            vec((CHUNKS, GROUP * 128, 512), BF16),
            vec((CHUNKS, BOTH, 512), BF16),
            vec((CHUNKS, BOTH, 512), BF16),
            vec((CHUNKS, GROUP * 128, 384), BF16),
            vec((CHUNKS, BOTH, 384), BF16),
            vec((CHUNKS, BOTH, 384), BF16),
            vec((HEADS, 64, 128), F32),
            vec((256, 1024), BF16),
            vec((HEADS * 8, 128), F32),
            vec((HEADS * 8, 128), F32),
            vec((GROUP, 64, 128), F32),
            vec((BOTH, GROUP * 128), BF16),
            vec((BOTH, GROUP * 128), BF16),
            vec((GROUP, 128, 128 + BOTH), BF16),
            vec((GROUP, 128, 128 + BOTH), BF16),
            vec((8, 8, 128), F32),
            vec((16, 8, 128), F32),
            vec((8, 8, 128), F32),
            vec((16, 256), jnp.int32),
            vec((HEADS, 512), F32),
            pltpu.SMEM((2,), jnp.int32),
            pltpu.SMEM((2, HEADS), F32),
            dma((4,)),
            dma((6,)),
            dma((2, CHUNKS)),
            dma((2, CHUNKS)),
            dma((2, CHUNKS)),
            dma((2, CHUNKS)),
            dma((2,)),
            dma((15,)),
            dma((15,)),
            dma((7,)),
            dma((7,)),
            dma((15,)),
            dma((15,)),
            dma((3, CHUNKS)),
        ],
        compiler_params=pltpu.CompilerParams(
            collective_id=0, has_side_effects=True, vmem_limit_bytes=60 * 2**20
        ),
        name="exchange_and_grads",
    )(*fields, land, shifts, first, offset.reshape(1, 512), second.T, keybias)
    gq, gk, gv, gfirst, goffset, gsecond, gkey = pl.pallas_call(
        last_kernel,
        out_shape=results,
        in_specs=[hbm] * 7,
        out_specs=(hbm,) * 7,
        scratch_shapes=[vec(r.shape, r.dtype) for r in results] + [dma((2, 16))],
        compiler_params=pltpu.CompilerParams(vmem_limit_bytes=60 * 2**20),
        name="write_and_reduce",
    )(*outs)
    return (
        gq.reshape(shape),
        gk.reshape(shape),
        gv.reshape(shape),
        gfirst,
        goffset.reshape(512),
        gsecond.T,
        gkey,
    )


def solution(mesh):
    field = P("dp", None, "space", "tensor")
    second = P(None, "tensor")
    return jax.shard_map(
        on_device,
        mesh=mesh,
        in_specs=(field,) * 4 + (P(), P(), P(), P(), second, second),
        out_specs=(field,) * 3 + (P(), P(), second, second),
        check_vma=False,
    )
```

```python
import jax
import jax.numpy as jnp
from jax import lax
from jax.experimental import pallas as pl
from jax.experimental.pallas import tpu as pltpu
from jax.sharding import PartitionSpec as P

MESH = pl.DeviceIdType.MESH
MASKED = -1000000000.0
LOG2E = 1.4426950408889634
HEADS = 20
GROUP = 4
CHUNKS = HEADS // GROUP
LANES = GROUP * 128
ROOM = 9
SIDE = ROOM * 16
BOTH = 2 * SIDE
EARLY = 3
BF16 = jnp.bfloat16
F32 = jnp.float32
HIGHEST = lax.Precision.HIGHEST


def iota(shape, dim):
    return lax.broadcasted_iota(jnp.int32, shape, dim)


def onehot(cond):
    return jnp.where(cond, 1.0, 0.0).astype(BF16)


def dot(a, b, ca, cb, precision=None):
    return lax.dot_general(
        a, b, (((ca,), (cb,)), ((), ())), preferred_element_type=F32, precision=precision
    )


def squash(t):
    t = t.astype(F32)
    size = jnp.log2(1.0 + jnp.abs(t)) / 3.0
    return jnp.where(t < 0, -size, size)


def hidden_before(first, offset):
    n = iota((256, 1), 0)
    dy, dx = n // 16, n % 16
    cy = squash(jnp.where(dy >= 8, dy - 16, dy))
    cx = squash(jnp.where(dx >= 8, dx - 16, dx))
    return cy * first[0:1, :] + cx * first[1:2, :] + offset, cy, cx


def used_bins(rows):
    n = iota((rows, 256), 1)
    return (n // 16 != 8) & (n % 16 != 8)


def three_parts(x):
    a = x.astype(BF16)
    rest = x - a.astype(F32)
    b = rest.astype(BF16)
    c = (rest - b.astype(F32)).astype(BF16)
    return jnp.concatenate([a, b, c], axis=0)


def two_parts(x):
    a = x.astype(BF16)
    return a, (x - a.astype(F32)).astype(BF16)


def west_heads(shift):
    return jnp.where(shift <= 2, 4, jnp.where(shift >= 6, 0, 6 - shift))


def block_of(head, column, shift, west):
    return jnp.where(
        head < west, head * shift + column, ROOM + (head - west) * (8 - shift) + column - shift
    )


def patch_code(head, n, shift, west):
    lat, column = n // 8, n % 8
    leaves = (head < west) == (column < shift)
    return jnp.where(leaves, block_of(head, column, shift, west) * 16 + lat, -1)


def window_place(head, w, shift, lat_shift, west):
    lat = (lat_shift + w // 8) % 16
    column = w % 8 + shift
    over = column >= 8
    return over == (head < west), jnp.where(over, column - 8, column), lat


def main_kernel(
    q_ref,
    k_ref,
    v_ref,
    d_ref,
    land_hbm,
    shifts_hbm,
    first_hbm,
    offset_hbm,
    second_hbm,
    keybias_hbm,
    gq_hbm,
    gk_hbm,
    gv_hbm,
    gfirst_ref,
    goffset_ref,
    gsecond_ref,
    gkey_ref,
    out_ref,
    sums_ref,
    seconds_ref,
    layer_ref,
    hidden_ref,
    slope_ref,
    merged_ref,
    probs_ref,
    dscores_ref,
    held,
    own,
    packed,
    lent,
    window,
    far,
    arrived,
    bias,
    expand,
    rows,
    land_rows,
    is_land,
    pack_in,
    pack_back,
    merge,
    place,
    table_part,
    near_part,
    z_part,
    land_ref,
    second_ref,
    shifts_ref,
    keybias_ref,
    load_sem,
    small_sem,
    in_send,
    in_recv,
    back_send,
    back_recv,
    second_sem,
    near_send,
    near_recv,
    z_send,
    z_recv,
    xy_send,
    xy_recv,
    out_sem,
    round_sem,
):
    y = lax.axis_index("dp")
    sp = lax.axis_index("space")
    t = lax.axis_index("tensor")
    core, z, x_lo = sp % 2, (sp // 2) % 8, sp // 16
    x = t * 2 + x_lo
    west_id = {"space": (sp + 31) % 32}
    east_id = {"space": (sp + 1) % 32}
    slow_id = {"space": (sp + 31 + 2 * core) % 32}
    near = []
    for k in sorted(range(1, 16), key=lambda k: -(k // 8 + 2 - abs((k // 2) % 4 - 2))):
        xx, yy, cc = (x_lo + k // 8) % 2, (y + (k // 2) % 4) % 4, (core + k) % 2
        near.append((xx * 4 + yy, {"dp": yy, "space": xx * 16 + z * 2 + cc}))
    z_ids = [{"space": x_lo * 16 + ((z + k) % 8) * 2 + core} for k in (4, 3, 5, 2, 6, 1, 7)]
    xy_ids = []
    for k in sorted(range(1, 16), key=lambda k: -(4 - abs(k // 4 - 2) - abs(k % 4 - 2))):
        xx, yy = (x + k // 4) % 4, (y + k % 4) % 4
        xy_ids.append({"dp": yy, "space": (xx % 2) * 16 + z * 2 + core, "tensor": xx // 2})
    other_ids = []
    for k in range(8):
        xx, yy = (x_lo + k // 4) % 2, (y + k % 4) % 4
        other_ids.append({"dp": yy, "space": xx * 16 + z * 2 + core, "tensor": 1 - t})
    tensor_id = {"tensor": 1 - t}
    core_id = {"space": sp + 1 - 2 * core}

    fields = (q_ref, k_ref, v_ref, d_ref)
    small = [
        pltpu.make_async_copy(a, b, small_sem.at[i])
        for i, (a, b) in enumerate(
            (
                (shifts_hbm, shifts_ref),
                (land_hbm, land_ref),
                (first_hbm, layer_ref.at[pl.ds(0, 2)]),
                (offset_hbm, layer_ref.at[pl.ds(2, 1)]),
                (second_hbm, second_ref),
                (keybias_hbm, keybias_ref),
            )
        )
    ]
    loads = [pltpu.make_async_copy(ref, held.at[a], load_sem.at[a]) for a, ref in enumerate(fields)]
    small[0].start()
    for copy in loads:
        copy.start()
    for copy in small[1:]:
        copy.start()

    steps = [slow_id, core_id]
    steps += [{"space": x_lo * 16 + ((z + k) % 8) * 2 + core} for k in (1, 7)]
    steps += [{"dp": (y + k) % 4} for k in (1, 3)]
    for k in (1, 3):
        xx = (x + k) % 4
        steps.append({"space": (xx % 2) * 16 + z * 2 + core, "tensor": xx // 2})
    barrier = pltpu.get_barrier_semaphore()
    for to in steps:
        pl.semaphore_signal(barrier, inc=1, device_id=to, device_id_type=MESH)

    def tell(round_at):
        for to in steps:
            pl.semaphore_signal(
                round_sem.at[round_at], inc=1, device_id=to, device_id_type=MESH
            )

    def hear(round_at):
        pl.semaphore_wait(round_sem.at[round_at], len(steps))

    def side_rows(side):
        return pl.ds(side * SIDE, SIDE)

    def in_copy(side, c):
        return pltpu.make_async_remote_copy(
            src_ref=packed.at[c, side_rows(side)],
            dst_ref=lent.at[c, side_rows(side)],
            send_sem=in_send.at[side, c],
            recv_sem=in_recv.at[side, c],
            device_id=east_id if side else west_id,
            device_id_type=MESH,
        )

    def back_copy(side, c):
        return pltpu.make_async_remote_copy(
            src_ref=far.at[c, side_rows(side)],
            dst_ref=arrived.at[c, side_rows(side)],
            send_sem=back_send.at[side, c],
            recv_sem=back_recv.at[side, c],
            device_id=west_id if side else east_id,
            device_id_type=MESH,
        )

    second_copy = pltpu.make_async_remote_copy(
        src_ref=second_hbm,
        dst_ref=seconds_ref.at[t],
        send_sem=second_sem.at[0],
        recv_sem=second_sem.at[1],
        device_id=tensor_id,
        device_id_type=MESH,
    )

    small[0].wait()
    lat_shift, shift = shifts_ref[0], shifts_ref[1]
    west = west_heads(shift)
    e = iota((1, GROUP * 128), 1)
    code = patch_code(e // 128, e % 128, shift, west)
    pack_in[...] = onehot(iota((BOTH, GROUP * 128), 0) == code)

    def pack(c):
        for i in range(GROUP):
            lanes = pl.ds(pl.multiple_of(c * LANES, LANES) + 128 * i, 128)
            for a in range(4):
                own[c, 128 * i : 128 * i + 128, 128 * a : 128 * a + 128] = held[
                    a, :, :, lanes
                ].reshape(128, 128)
        packed[c] = dot(pack_in[...], own[c], 1, 0).astype(BF16)

    for copy in loads:
        copy.wait()
    pack(0)
    pl.semaphore_wait(barrier, len(steps))
    for side in range(2):
        in_copy(side, 0).start()
    tell(0)

    @pl.loop(1, CHUNKS)
    def _(c):
        pack(c)
        for side in range(2):
            in_copy(side, c).start()

    for copy in small[1:]:
        copy.wait()
    seconds_ref[t] = second_ref[...]

    borrowed, column, lat = window_place(e // 128, e % 128, shift, lat_shift, west)
    code = jnp.where(borrowed, block_of(e // 128, column, shift, west) * 16 + lat, -1)
    pack_back[...] = onehot(iota((BOTH, GROUP * 128), 0) == code)
    for i in range(GROUP):
        n, target = iota((128, 1), 0), iota((128, 128 + BOTH), 1)
        borrowed, column, lat = window_place(i, n, shift, lat_shift, west)
        code = block_of(i, column, shift, west) * 16 + lat
        merge[i] = onehot(target == jnp.where(borrowed, 128 + code, lat * 8 + column))
        code = patch_code(i, n, shift, west)
        row = (n // 8 + 16 - lat_shift) % 16
        here = row * 8 + (n % 8 + 8 - shift) % 8
        place[i] = onehot(target == jnp.where(code >= 0, 128 + code, here))

    pre, _, _ = hidden_before(layer_ref[0:2, :], layer_ref[2:3, :])
    logits = dot(second_ref[...], jnp.maximum(pre, 0.0), 1, 1, HIGHEST)
    table = jnp.where(used_bins(HEADS), 16.0 * jax.nn.sigmoid(logits), 0.0)
    table = three_parts(jnp.concatenate([table, jnp.zeros((4, 256), F32)], axis=0))
    for cj in range(8):
        b, l = iota((128, 256), 1), iota((128, 256), 0)
        here = (b == (l // 8) * 16 + (l % 8 - cj + 16) % 16) | (b == 8) | (b == 24)
        expand[cj * 128 : (cj + 1) * 128, :] = onehot(here)
        b, l = iota((256, 128), 0), iota((256, 128), 1)
        here = b == (l // 8) * 16 + (l % 8 - cj + 16) % 16
        wide = dot(table, onehot(here), 1, 0)
        wide = wide[0:24] + wide[24:48] + wide[48:72]
        rows[pl.ds(cj, HEADS, stride=8), :] = wide[0:HEADS]

    land = land_ref[...].astype(F32).astype(BF16)
    j, l = iota((64, 128), 0), iota((64, 128), 1)
    lands = []
    for side in range(2):
        g, cols = iota((256, 128), 0), iota((256, 128), 1)
        first_col = (sp + 31 * side) * 8 + shift
        land_cols = dot(land, onehot(g == (first_col + cols) % 256), 1, 0).astype(BF16)
        halves = []
        for blk in range(2):
            jj, lat = iota((64, 16), 0), iota((64, 16), 1)
            pick = onehot(lat == (lat_shift + jj // 8 + 8 * blk) % 16)
            spread = dot(pick, land_cols, 1, 0)
            halves.append(jnp.sum(jnp.where(l == j % 8, spread, 0.0), axis=1, keepdims=True))
        lands.append(jnp.where(l < 64, halves[0], halves[1]))
    for i in range(GROUP):
        is_land[i] = jnp.where(i < west, lands[0], lands[1])
    apart = (l >= 64) & ((j // 8 < 8 - lat_shift) != ((l % 64) // 8 < 8 - lat_shift))
    masked = jnp.where(apart, MASKED * LOG2E, 0.0)

    @pl.loop(0, CHUNKS)
    def _(c):
        lane = iota((8, 128), 1)
        for i in range(GROUP):
            h = c * GROUP + i
            one = rows[pl.ds(pl.multiple_of(h * 8, 8), 8), :]
            low, high = keybias_ref[0, h] * LOG2E, keybias_ref[1, h] * LOG2E
            for rj in range(8):
                left = pltpu.roll(one, 8 * rj, 1) if rj else one
                right = pltpu.roll(one, 8 * rj + 64, 1)
                at = slice(8 * rj, 8 * rj + 8)
                key = jnp.where(is_land[i, at] > 0.5, high, low) + masked[at]
                bias[h, at, :] = jnp.where(lane < 64, left, right) * LOG2E + key

    hear(0)
    tell(1)
    second_copy.start()
    scale = 128.0 ** -0.5

    front = iota((64, 128), 1) < 64
    lane8 = iota((8, 128), 1)

    def paired(x):
        return jnp.where(front, x[0:64], x[64:128])

    def split(x):
        return jnp.concatenate([jnp.where(front, x, 0.0), jnp.where(front, 0.0, x)], axis=0)

    def receive(c):
        for side in range(2):
            in_copy(side, c).wait_recv()

    def give_back(c):
        for side in range(2):
            back_copy(side, c).start()

    def attention(c):
        theirs = lent[c]
        merged = []
        for i in range(GROUP):
            both = jnp.concatenate([own[c, 128 * i : 128 * i + 128, :], theirs], axis=0)
            whole = dot(merge[i], both, 1, 0).astype(BF16)
            merged_ref[c % 2, i] = whole
            merged.append([whole[:, 128 * a : 128 * a + 128] for a in range(4)])
        scores = [paired(dot(f[1], f[0], 1, 1)) for f in merged]
        dprobs = [paired(dot(f[2], f[3], 1, 1)) for f in merged]
        for i in range(GROUP):
            h = c * GROUP + i
            sc = scores[i] * (scale * LOG2E) + bias[h]
            e = jnp.exp2(sc - jnp.max(sc, axis=0, keepdims=True))
            p = e * (1.0 / jnp.sum(e, axis=0, keepdims=True))
            pd = p * dprobs[i]
            ds = pd - p * jnp.sum(pd, axis=0, keepdims=True)
            probs_ref[c % 2, i] = split(p).astype(BF16)
            dscores_ref[c % 2, i] = split(ds).astype(BF16)
            acc = jnp.zeros((8, 128), F32)
            land_acc = jnp.zeros((8, 128), F32)
            for rj in range(8):
                at = slice(8 * rj, 8 * rj + 8)
                part = ds[at]
                land_acc += part * is_land[i, at]
                both = jnp.where(lane8 < 64, part + pltpu.roll(part, 64, 1), 0.0)
                acc += pltpu.roll(both, 128 - 8 * rj, 1) if rj else both
            at = pl.ds(pl.multiple_of(h * 8, 8), 8)
            rows[at, :] = acc
            land_rows[at, :] = land_acc

    def gradients(c):
        for i in range(GROUP):
            f, at = merged_ref[c % 2, i], slice(128 * i, 128 * i + 128)
            p_low, ds_low = probs_ref[c % 2, i], dscores_ref[c % 2, i]
            window[c, at, 0:128] = (dot(ds_low, f[:, 128:256], 0, 0) * scale).astype(BF16)
            window[c, at, 128:256] = (dot(ds_low, f[:, 0:128], 1, 0) * scale).astype(BF16)
            window[c, at, 256:384] = dot(p_low, f[:, 384:512], 1, 0).astype(BF16)
        far[c] = dot(pack_back[...], window[c], 1, 0).astype(BF16)

    receive(0)
    attention(0)
    hear(1)
    tell(2)

    @pl.loop(1, CHUNKS - 1)
    def _(c):
        receive(c)
        attention(c)
        gradients(c - 1)

        @pl.when(c <= EARLY)
        def _():
            give_back(c - 1)

    receive(CHUNKS - 1)
    attention(CHUNKS - 1)
    hear(2)

    pad = jnp.zeros((4, 1024), F32)
    flat = jnp.concatenate([rows[pl.ds(cj, HEADS, stride=8), :] for cj in range(8)], axis=1)
    land_flat = jnp.concatenate(
        [land_rows[pl.ds(cj, HEADS, stride=8), :] for cj in range(8)], axis=1
    )
    stacked = three_parts(jnp.concatenate([flat, pad, land_flat, pad], axis=0))
    binned = dot(stacked, expand[...], 1, 0)
    binned = binned[0:48] + binned[48:96] + binned[96:144]
    binned = jnp.where(iota((24, 256), 1) == 24, binned[24:48], binned[0:24])
    for i in range(6):
        table_part[i] = binned[(i // 2) * 8 : (i // 2) * 8 + 8, (i % 2) * 128 : (i % 2) * 128 + 128]
    table_part[6:8] = jnp.zeros((2, 8, 128), F32)

    def exchange(pieces):
        return [
            pltpu.make_async_remote_copy(
                src_ref=src,
                dst_ref=dst,
                send_sem=send.at[i],
                recv_sem=recv.at[i],
                device_id=to,
                device_id_type=MESH,
            )
            for i, (src, dst, send, recv, to) in enumerate(pieces)
        ]

    def out_copies(c):
        lanes = pl.ds(pl.multiple_of(c * LANES, LANES), LANES)
        return [
            pltpu.make_async_copy(out_ref.at[a, :, :, lanes], out.at[:, :, lanes], out_sem.at[a, c])
            for a, out in enumerate((gq_hbm, gk_hbm, gv_hbm))
        ]

    def finish(c):
        for side in range(2):
            back_copy(side, c).wait_recv()
        theirs = arrived[c]
        for i in range(GROUP):
            lanes = pl.ds(pl.multiple_of(c * LANES, LANES) + 128 * i, 128)
            both = jnp.concatenate([window[c, 128 * i : 128 * i + 128, :], theirs], axis=0)
            whole = dot(place[i], both, 1, 0).astype(BF16)
            for a in range(3):
                out_ref[a, :, :, lanes] = whole[:, 128 * a : 128 * a + 128].reshape(16, 8, 128)
        for copy in out_copies(c):
            copy.start()

    slot = x_lo * 4 + y
    copies = exchange(
        [(table_part.at[i], near_part.at[slot * 2 + core], near_send, near_recv, to) for i, to in near]
    )
    for copy in copies:
        copy.start()
    near_part[slot * 2 + core] = table_part[slot]
    gradients(CHUNKS - 2)
    gradients(CHUNKS - 1)
    second_copy.wait()
    pre, cy, cx = hidden_before(layer_ref[0:2, :], layer_ref[2:3, :])
    hidden = jnp.maximum(pre, 0.0)
    hidden_ref[0], hidden_ref[1] = two_parts(hidden)
    sent = copies
    for copy in copies:
        copy.wait_recv()
    mine = near_part[0]
    for i in range(1, 16):
        mine = mine + near_part[i]

    z_part[z] = mine
    copies = exchange([(z_part.at[z], z_part.at[z], z_send, z_recv, to) for to in z_ids])
    for copy in copies:
        copy.start()

    for c in range(EARLY, CHUNKS):
        give_back(c)
    for half in range(2):
        p = jax.nn.sigmoid(dot(seconds_ref[half], hidden, 1, 1, HIGHEST))
        slope_ref[half] = jnp.where(used_bins(HEADS), 16.0 * p * (1.0 - p), 0.0)

    @pl.loop(0, 2)
    def _(c):
        finish(c)

    sent = sent + copies
    for copy in copies:
        copy.wait_recv()
    mine = z_part[0]
    for i in range(1, 8):
        mine = mine + z_part[i]

    sums_ref[x * 4 + y] = mine
    here = sums_ref.at[x * 4 + y]
    copies = exchange([(here, here, xy_send, xy_recv, to) for to in xy_ids])
    for copy in copies:
        copy.start()

    @pl.loop(2, CHUNKS)
    def _(c):
        finish(c)

    @pl.loop(0, CHUNKS)
    def _(c):
        for side in range(2):
            in_copy(side, c).wait_send()
            back_copy(side, c).wait_send()

    seconds = jnp.concatenate([seconds_ref[0], seconds_ref[1]], axis=0)
    seconds_high, seconds_low = two_parts(seconds)
    seconds_three = jnp.concatenate([seconds_high, seconds_high, seconds_low], axis=0)
    sent = sent + copies
    for copy in copies:
        copy.wait_recv()

    def bins(half):
        strips = [
            jnp.concatenate([sums_ref[half * 8 + 2 * i], sums_ref[half * 8 + 2 * i + 1]], axis=1)
            for i in range(3)
        ]
        return jnp.concatenate(strips, axis=0)

    pulled = [bins(half)[0:HEADS] * slope_ref[half] for half in range(2)]
    high, low = two_parts(jnp.where(t == 0, pulled[0], pulled[1]))
    gsecond = dot(jnp.concatenate([high, low], axis=0), hidden_ref[0], 1, 0)
    gsecond_ref[...] = (
        gsecond[0:HEADS] + gsecond[HEADS : 2 * HEADS] + dot(high, hidden_ref[1], 1, 0)
    )
    high, low = two_parts(jnp.concatenate(pulled, axis=0))
    ghidden = dot(jnp.concatenate([high, low, high], axis=0), seconds_three, 0, 0)
    ghidden = jnp.where(pre > 0.0, ghidden, 0.0)
    gfirst_ref[0:1, :] = jnp.sum(cy * ghidden, axis=0, keepdims=True)
    gfirst_ref[1:2, :] = jnp.sum(cx * ghidden, axis=0, keepdims=True)
    goffset_ref[...] = jnp.sum(ghidden, axis=0, keepdims=True)
    r, n = iota((8, 256), 0), iota((8, 256), 1)
    pick = jnp.where(n == 24, jnp.where(r == 0, -1.0, 1.0), jnp.where((n == 8) & (r == 0), 1.0, 0.0))
    keys = dot(pick, jnp.where(t == 0, bins(0), bins(1)), 1, 1, HIGHEST)
    gkey_ref[...] = keys[0:2, 0:HEADS]
    for copy in sent:
        copy.wait_send()

    @pl.loop(0, CHUNKS)
    def _(c):
        for copy in out_copies(c):
            copy.wait()


def last_kernel(*refs):
    n = len(refs) // 3
    given, placed, held, sem = refs[:n], refs[n : 2 * n], refs[2 * n : 3 * n], refs[3 * n]
    pieces = [(i, pl.ds(4 * part, 4)) for part in range(4) for i in range(3)]
    pieces += [(i, slice(None)) for i in range(3, n)]
    loads, copies = [], []
    for at, (i, part) in enumerate(pieces):
        here = held[i].at[part]
        loads.append(pltpu.make_async_copy(given[i].at[part], here, sem.at[0, at]))
        copies.append(pltpu.make_async_copy(here, placed[i].at[part], sem.at[1, at]))
    for load in loads:
        load.start()
    for load, copy in zip(loads, copies):
        load.wait()
        copy.start()
    for copy in copies:
        copy.wait()


def on_device(q, k, v, d, land, shifts, first, offset, second, keybias):
    shape = q.shape
    field = (16, 8, HEADS * 128)
    fields = [a.reshape(field) for a in (q, k, v, d)]
    vmem = pl.BlockSpec(memory_space=pltpu.VMEM)
    hbm = pl.BlockSpec(memory_space=pltpu.HBM)
    dma = pltpu.SemaphoreType.DMA
    vec = pltpu.VMEM
    results = (jax.ShapeDtypeStruct(field, BF16),) * 3 + (
        jax.ShapeDtypeStruct((2, 512), F32),
        jax.ShapeDtypeStruct((1, 512), F32),
        jax.ShapeDtypeStruct((HEADS, 512), F32),
        jax.ShapeDtypeStruct((2, HEADS), F32),
    )
    outs = pl.pallas_call(
        main_kernel,
        out_shape=results,
        in_specs=[hbm] * 10,
        out_specs=(hbm,) * 3 + (vmem,) * 4,
        scratch_shapes=[
            vec((3,) + field, BF16),
            vec((16, 8, 128), F32),
            vec((2, HEADS, 512), F32),
            vec((3, 512), F32),
            vec((2, 256, 512), BF16),
            vec((2, HEADS, 256), F32),
            vec((2, GROUP, 128, 512), BF16),
            vec((2, GROUP, 128, 128), BF16),
            vec((2, GROUP, 128, 128), BF16),
            vec((4,) + field, BF16),
            vec((CHUNKS, GROUP * 128, 512), BF16),
            vec((CHUNKS, BOTH, 512), BF16),
            vec((CHUNKS, BOTH, 512), BF16),
            vec((CHUNKS, GROUP * 128, 384), BF16),
            vec((CHUNKS, BOTH, 384), BF16),
            vec((CHUNKS, BOTH, 384), BF16),
            vec((HEADS, 64, 128), F32),
            vec((1024, 256), BF16),
            vec((HEADS * 8, 128), F32),
            vec((HEADS * 8, 128), F32),
            vec((GROUP, 64, 128), F32),
            vec((BOTH, GROUP * 128), BF16),
            vec((BOTH, GROUP * 128), BF16),
            vec((GROUP, 128, 128 + BOTH), BF16),
            vec((GROUP, 128, 128 + BOTH), BF16),
            vec((8, 8, 128), F32),
            vec((16, 8, 128), F32),
            vec((8, 8, 128), F32),
            vec((16, 256), jnp.int32),
            vec((HEADS, 512), F32),
            pltpu.SMEM((2,), jnp.int32),
            pltpu.SMEM((2, HEADS), F32),
            dma((4,)),
            dma((6,)),
            dma((2, CHUNKS)),
            dma((2, CHUNKS)),
            dma((2, CHUNKS)),
            dma((2, CHUNKS)),
            dma((2,)),
            dma((15,)),
            dma((15,)),
            dma((7,)),
            dma((7,)),
            dma((15,)),
            dma((15,)),
            dma((3, CHUNKS)),
            pltpu.SemaphoreType.REGULAR((3,)),
        ],
        compiler_params=pltpu.CompilerParams(
            collective_id=0, has_side_effects=True, vmem_limit_bytes=60 * 2**20
        ),
        name="exchange_and_grads",
    )(*fields, land, shifts, first, offset.reshape(1, 512), second.T, keybias)
    gq, gk, gv, gfirst, goffset, gsecond, gkey = pl.pallas_call(
        last_kernel,
        out_shape=results,
        in_specs=[hbm] * 7,
        out_specs=(hbm,) * 7,
        scratch_shapes=[vec(r.shape, r.dtype) for r in results] + [dma((2, 16))],
        compiler_params=pltpu.CompilerParams(vmem_limit_bytes=60 * 2**20),
        name="write_and_reduce",
    )(*outs)
    return (
        gq.reshape(shape),
        gk.reshape(shape),
        gv.reshape(shape),
        gfirst,
        goffset.reshape(512),
        gsecond.T,
        gkey,
    )


def solution(mesh):
    field = P("dp", None, "space", "tensor")
    second = P(None, "tensor")
    return jax.shard_map(
        on_device,
        mesh=mesh,
        in_specs=(field,) * 4 + (P(), P(), P(), P(), second, second),
        out_specs=(field,) * 3 + (P(), P(), second, second),
        check_vma=False,
    )
```

```python
import jax
import jax.numpy as jnp
from jax import lax
from jax.experimental import pallas as pl
from jax.experimental.pallas import tpu as pltpu
from jax.sharding import PartitionSpec as P

MESH = pl.DeviceIdType.MESH
MASKED = -1000000000.0
LOG2E = 1.4426950408889634
HEADS = 20
GROUP = 4
CHUNKS = HEADS // GROUP
LANES = GROUP * 128
ROOM = 9
SIDE = ROOM * 16
BOTH = 2 * SIDE
EARLY = 2
BF16 = jnp.bfloat16
F32 = jnp.float32
HIGHEST = lax.Precision.HIGHEST


def iota(shape, dim):
    return lax.broadcasted_iota(jnp.int32, shape, dim)


def onehot(cond):
    return jnp.where(cond, 1.0, 0.0).astype(BF16)


def dot(a, b, ca, cb, precision=None):
    return lax.dot_general(
        a, b, (((ca,), (cb,)), ((), ())), preferred_element_type=F32, precision=precision
    )


def squash(t):
    t = t.astype(F32)
    size = jnp.log2(1.0 + jnp.abs(t)) / 3.0
    return jnp.where(t < 0, -size, size)


def hidden_before(first, offset):
    n = iota((256, 1), 0)
    dy, dx = n // 16, n % 16
    cy = squash(jnp.where(dy >= 8, dy - 16, dy))
    cx = squash(jnp.where(dx >= 8, dx - 16, dx))
    return cy * first[0:1, :] + cx * first[1:2, :] + offset, cy, cx


def used_bins(rows):
    n = iota((rows, 256), 1)
    return (n // 16 != 8) & (n % 16 != 8)


def three_parts(x):
    a = x.astype(BF16)
    rest = x - a.astype(F32)
    b = rest.astype(BF16)
    c = (rest - b.astype(F32)).astype(BF16)
    return jnp.concatenate([a, b, c], axis=0)


def two_parts(x):
    a = x.astype(BF16)
    return a, (x - a.astype(F32)).astype(BF16)


def west_heads(shift):
    return jnp.where(shift <= 2, 4, jnp.where(shift >= 6, 0, 6 - shift))


def block_of(head, column, shift, west):
    return jnp.where(
        head < west, head * shift + column, ROOM + (head - west) * (8 - shift) + column - shift
    )


def patch_code(head, n, shift, west):
    lat, column = n // 8, n % 8
    leaves = (head < west) == (column < shift)
    return jnp.where(leaves, block_of(head, column, shift, west) * 16 + lat, -1)


def window_place(head, w, shift, lat_shift, west):
    lat = (lat_shift + w // 8) % 16
    column = w % 8 + shift
    over = column >= 8
    return over == (head < west), jnp.where(over, column - 8, column), lat


def main_kernel(
    q_ref,
    k_ref,
    v_ref,
    d_ref,
    land_hbm,
    shifts_hbm,
    first_hbm,
    offset_hbm,
    second_hbm,
    keybias_hbm,
    gq_hbm,
    gk_hbm,
    gv_hbm,
    gfirst_ref,
    goffset_ref,
    gsecond_ref,
    gkey_ref,
    out_ref,
    sums_ref,
    seconds_ref,
    layer_ref,
    hidden_ref,
    slope_ref,
    merged_ref,
    probs_ref,
    dscores_ref,
    held,
    own,
    packed,
    lent,
    window,
    far,
    arrived,
    bias,
    expand,
    rows,
    land_rows,
    is_land,
    pack_in,
    pack_back,
    merge,
    place,
    table_part,
    near_part,
    z_part,
    land_ref,
    second_ref,
    shifts_ref,
    keybias_ref,
    load_sem,
    small_sem,
    in_send,
    in_recv,
    back_send,
    back_recv,
    second_sem,
    near_send,
    near_recv,
    z_send,
    z_recv,
    xy_send,
    xy_recv,
    out_sem,
    round_sem,
):
    y = lax.axis_index("dp")
    sp = lax.axis_index("space")
    t = lax.axis_index("tensor")
    core, z, x_lo = sp % 2, (sp // 2) % 8, sp // 16
    x = t * 2 + x_lo
    west_id = {"space": (sp + 31) % 32}
    east_id = {"space": (sp + 1) % 32}
    slow_id = {"space": (sp + 31 + 2 * core) % 32}
    near = []
    for k in sorted(range(1, 16), key=lambda k: -(k // 8 + 2 - abs((k // 2) % 4 - 2))):
        xx, yy, cc = (x_lo + k // 8) % 2, (y + (k // 2) % 4) % 4, (core + k) % 2
        near.append((xx * 4 + yy, {"dp": yy, "space": xx * 16 + z * 2 + cc}))
    z_ids = [{"space": x_lo * 16 + ((z + k) % 8) * 2 + core} for k in (4, 3, 5, 2, 6, 1, 7)]
    xy_ids = []
    for k in sorted(range(1, 16), key=lambda k: -(4 - abs(k // 4 - 2) - abs(k % 4 - 2))):
        xx, yy = (x + k // 4) % 4, (y + k % 4) % 4
        xy_ids.append({"dp": yy, "space": (xx % 2) * 16 + z * 2 + core, "tensor": xx // 2})
    other_ids = []
    for k in range(8):
        xx, yy = (x_lo + k // 4) % 2, (y + k % 4) % 4
        other_ids.append({"dp": yy, "space": xx * 16 + z * 2 + core, "tensor": 1 - t})
    tensor_id = {"tensor": 1 - t}
    core_id = {"space": sp + 1 - 2 * core}

    fields = (q_ref, k_ref, v_ref, d_ref)
    small = [
        pltpu.make_async_copy(a, b, small_sem.at[i])
        for i, (a, b) in enumerate(
            (
                (shifts_hbm, shifts_ref),
                (land_hbm, land_ref),
                (first_hbm, layer_ref.at[pl.ds(0, 2)]),
                (offset_hbm, layer_ref.at[pl.ds(2, 1)]),
                (second_hbm, second_ref),
                (keybias_hbm, keybias_ref),
            )
        )
    ]
    loads = []
    for part, lanes in enumerate((pl.ds(0, LANES), pl.ds(LANES, (CHUNKS - 1) * LANES))):
        loads.append(
            [
                pltpu.make_async_copy(
                    ref.at[:, :, lanes], held.at[a, :, :, lanes], load_sem.at[part, a]
                )
                for a, ref in enumerate(fields)
            ]
        )
    small[0].start()
    for copy in loads[0]:
        copy.start()

    steps = [slow_id, core_id]
    steps += [{"space": x_lo * 16 + ((z + k) % 8) * 2 + core} for k in (1, 7)]
    steps += [{"dp": (y + k) % 4} for k in (1, 3)]
    for k in (1, 3):
        xx = (x + k) % 4
        steps.append({"space": (xx % 2) * 16 + z * 2 + core, "tensor": xx // 2})
    barrier = pltpu.get_barrier_semaphore()
    for to in steps:
        pl.semaphore_signal(barrier, inc=1, device_id=to, device_id_type=MESH)

    for copy in loads[1] + small[1:]:
        copy.start()

    def tell(round_at):
        for to in steps:
            pl.semaphore_signal(
                round_sem.at[round_at], inc=1, device_id=to, device_id_type=MESH
            )

    def hear(round_at):
        pl.semaphore_wait(round_sem.at[round_at], len(steps))

    def side_rows(side):
        return pl.ds(side * SIDE, SIDE)

    def in_copy(side, c):
        return pltpu.make_async_remote_copy(
            src_ref=packed.at[c, side_rows(side)],
            dst_ref=lent.at[c, side_rows(side)],
            send_sem=in_send.at[side, c],
            recv_sem=in_recv.at[side, c],
            device_id=east_id if side else west_id,
            device_id_type=MESH,
        )

    def back_copy(side, c):
        return pltpu.make_async_remote_copy(
            src_ref=far.at[c, side_rows(side)],
            dst_ref=arrived.at[c, side_rows(side)],
            send_sem=back_send.at[side, c],
            recv_sem=back_recv.at[side, c],
            device_id=west_id if side else east_id,
            device_id_type=MESH,
        )

    second_copy = pltpu.make_async_remote_copy(
        src_ref=second_hbm,
        dst_ref=seconds_ref.at[t],
        send_sem=second_sem.at[0],
        recv_sem=second_sem.at[1],
        device_id=tensor_id,
        device_id_type=MESH,
    )

    small[0].wait()
    lat_shift, shift = shifts_ref[0], shifts_ref[1]
    west = west_heads(shift)
    e = iota((1, GROUP * 128), 1)
    code = patch_code(e // 128, e % 128, shift, west)
    pack_in[...] = onehot(iota((BOTH, GROUP * 128), 0) == code)

    def pack(c):
        for i in range(GROUP):
            lanes = pl.ds(pl.multiple_of(c * LANES, LANES) + 128 * i, 128)
            for a in range(4):
                own[c, 128 * i : 128 * i + 128, 128 * a : 128 * a + 128] = held[
                    a, :, :, lanes
                ].reshape(128, 128)
        packed[c] = dot(pack_in[...], own[c], 1, 0).astype(BF16)

    for copy in loads[0]:
        copy.wait()
    pack(0)
    pl.semaphore_wait(barrier, len(steps))
    for side in range(2):
        in_copy(side, 0).start()
    tell(0)
    for copy in loads[1]:
        copy.wait()

    @pl.loop(1, CHUNKS)
    def _(c):
        pack(c)
        for side in range(2):
            in_copy(side, c).start()

    for copy in small[1:]:
        copy.wait()
    seconds_ref[t] = second_ref[...]

    borrowed, column, lat = window_place(e // 128, e % 128, shift, lat_shift, west)
    code = jnp.where(borrowed, block_of(e // 128, column, shift, west) * 16 + lat, -1)
    pack_back[...] = onehot(iota((BOTH, GROUP * 128), 0) == code)
    for i in range(GROUP):
        n, target = iota((128, 1), 0), iota((128, 128 + BOTH), 1)
        borrowed, column, lat = window_place(i, n, shift, lat_shift, west)
        code = block_of(i, column, shift, west) * 16 + lat
        merge[i] = onehot(target == jnp.where(borrowed, 128 + code, lat * 8 + column))
        code = patch_code(i, n, shift, west)
        row = (n // 8 + 16 - lat_shift) % 16
        here = row * 8 + (n % 8 + 8 - shift) % 8
        place[i] = onehot(target == jnp.where(code >= 0, 128 + code, here))

    pre, _, _ = hidden_before(layer_ref[0:2, :], layer_ref[2:3, :])
    logits = dot(second_ref[...], jnp.maximum(pre, 0.0), 1, 1, HIGHEST)
    table = jnp.where(used_bins(HEADS), 16.0 * jax.nn.sigmoid(logits), 0.0)
    table = three_parts(jnp.concatenate([table, jnp.zeros((4, 256), F32)], axis=0))
    for cj in range(8):
        b, l = iota((128, 256), 1), iota((128, 256), 0)
        here = (b == (l // 8) * 16 + (l % 8 - cj + 16) % 16) | (b == 8) | (b == 24)
        expand[cj * 128 : (cj + 1) * 128, :] = onehot(here)
        b, l = iota((256, 128), 0), iota((256, 128), 1)
        here = b == (l // 8) * 16 + (l % 8 - cj + 16) % 16
        wide = dot(table, onehot(here), 1, 0)
        wide = wide[0:24] + wide[24:48] + wide[48:72]
        rows[pl.ds(cj, HEADS, stride=8), :] = wide[0:HEADS]

    land = land_ref[...].astype(F32).astype(BF16)
    j, l = iota((64, 128), 0), iota((64, 128), 1)
    lands = []
    for side in range(2):
        g, cols = iota((256, 128), 0), iota((256, 128), 1)
        first_col = (sp + 31 * side) * 8 + shift
        land_cols = dot(land, onehot(g == (first_col + cols) % 256), 1, 0).astype(BF16)
        halves = []
        for blk in range(2):
            jj, lat = iota((64, 16), 0), iota((64, 16), 1)
            pick = onehot(lat == (lat_shift + jj // 8 + 8 * blk) % 16)
            spread = dot(pick, land_cols, 1, 0)
            halves.append(jnp.sum(jnp.where(l == j % 8, spread, 0.0), axis=1, keepdims=True))
        lands.append(jnp.where(l < 64, halves[0], halves[1]))
    for i in range(GROUP):
        is_land[i] = jnp.where(i < west, lands[0], lands[1])
    apart = (l >= 64) & ((j // 8 < 8 - lat_shift) != ((l % 64) // 8 < 8 - lat_shift))
    masked = jnp.where(apart, MASKED * LOG2E, 0.0)

    @pl.loop(0, CHUNKS)
    def _(c):
        lane = iota((8, 128), 1)
        for i in range(GROUP):
            h = c * GROUP + i
            one = rows[pl.ds(pl.multiple_of(h * 8, 8), 8), :]
            low, high = keybias_ref[0, h] * LOG2E, keybias_ref[1, h] * LOG2E
            for rj in range(8):
                left = pltpu.roll(one, 8 * rj, 1) if rj else one
                right = pltpu.roll(one, 8 * rj + 64, 1)
                at = slice(8 * rj, 8 * rj + 8)
                key = jnp.where(is_land[i, at] > 0.5, high, low) + masked[at]
                bias[h, at, :] = jnp.where(lane < 64, left, right) * LOG2E + key

    hear(0)
    tell(1)
    second_copy.start()
    scale = 128.0 ** -0.5

    front = iota((64, 128), 1) < 64
    lane8 = iota((8, 128), 1)

    def paired(x):
        return jnp.where(front, x[0:64], x[64:128])

    def split(x):
        return jnp.concatenate([jnp.where(front, x, 0.0), jnp.where(front, 0.0, x)], axis=0)

    def receive(c):
        for side in range(2):
            in_copy(side, c).wait_recv()

    def give_back(c):
        for side in range(2):
            back_copy(side, c).start()

    def attention(c):
        theirs = lent[c]
        merged = []
        for i in range(GROUP):
            both = jnp.concatenate([own[c, 128 * i : 128 * i + 128, :], theirs], axis=0)
            whole = dot(merge[i], both, 1, 0).astype(BF16)
            merged_ref[c % 2, i] = whole
            merged.append([whole[:, 128 * a : 128 * a + 128] for a in range(4)])
        scores = [paired(dot(f[1], f[0], 1, 1)) for f in merged]
        dprobs = [paired(dot(f[2], f[3], 1, 1)) for f in merged]
        for i in range(GROUP):
            h = c * GROUP + i
            sc = scores[i] * (scale * LOG2E) + bias[h]
            e = jnp.exp2(sc - jnp.max(sc, axis=0, keepdims=True))
            p = e * (1.0 / jnp.sum(e, axis=0, keepdims=True))
            pd = p * dprobs[i]
            ds = pd - p * jnp.sum(pd, axis=0, keepdims=True)
            probs_ref[c % 2, i] = split(p).astype(BF16)
            dscores_ref[c % 2, i] = split(ds).astype(BF16)
            acc = jnp.zeros((8, 128), F32)
            land_acc = jnp.zeros((8, 128), F32)
            for rj in range(8):
                at = slice(8 * rj, 8 * rj + 8)
                part = ds[at]
                land_acc += part * is_land[i, at]
                both = jnp.where(lane8 < 64, part + pltpu.roll(part, 64, 1), 0.0)
                acc += pltpu.roll(both, 128 - 8 * rj, 1) if rj else both
            at = pl.ds(pl.multiple_of(h * 8, 8), 8)
            rows[at, :] = acc
            land_rows[at, :] = land_acc

    def gradients(c):
        for i in range(GROUP):
            f, at = merged_ref[c % 2, i], slice(128 * i, 128 * i + 128)
            p_low, ds_low = probs_ref[c % 2, i], dscores_ref[c % 2, i]
            window[c, at, 0:128] = (dot(ds_low, f[:, 128:256], 0, 0) * scale).astype(BF16)
            window[c, at, 128:256] = (dot(ds_low, f[:, 0:128], 1, 0) * scale).astype(BF16)
            window[c, at, 256:384] = dot(p_low, f[:, 384:512], 1, 0).astype(BF16)
        far[c] = dot(pack_back[...], window[c], 1, 0).astype(BF16)

    receive(0)
    attention(0)
    hear(1)
    tell(2)

    @pl.loop(1, CHUNKS - 1)
    def _(c):
        receive(c)
        attention(c)
        gradients(c - 1)

        @pl.when(c <= EARLY)
        def _():
            give_back(c - 1)

    receive(CHUNKS - 1)
    attention(CHUNKS - 1)
    hear(2)

    pad = jnp.zeros((4, 1024), F32)
    flat = jnp.concatenate([rows[pl.ds(cj, HEADS, stride=8), :] for cj in range(8)], axis=1)
    land_flat = jnp.concatenate(
        [land_rows[pl.ds(cj, HEADS, stride=8), :] for cj in range(8)], axis=1
    )
    stacked = three_parts(jnp.concatenate([flat, pad, land_flat, pad], axis=0))
    binned = dot(stacked, expand[...], 1, 0)
    binned = binned[0:48] + binned[48:96] + binned[96:144]
    binned = jnp.where(iota((24, 256), 1) == 24, binned[24:48], binned[0:24])
    for i in range(6):
        table_part[i] = binned[(i // 2) * 8 : (i // 2) * 8 + 8, (i % 2) * 128 : (i % 2) * 128 + 128]
    table_part[6:8] = jnp.zeros((2, 8, 128), F32)

    def exchange(pieces):
        return [
            pltpu.make_async_remote_copy(
                src_ref=src,
                dst_ref=dst,
                send_sem=send.at[i],
                recv_sem=recv.at[i],
                device_id=to,
                device_id_type=MESH,
            )
            for i, (src, dst, send, recv, to) in enumerate(pieces)
        ]

    def out_copies(c):
        lanes = pl.ds(pl.multiple_of(c * LANES, LANES), LANES)
        return [
            pltpu.make_async_copy(out_ref.at[a, :, :, lanes], out.at[:, :, lanes], out_sem.at[a, c])
            for a, out in enumerate((gq_hbm, gk_hbm, gv_hbm))
        ]

    def finish(c):
        for side in range(2):
            back_copy(side, c).wait_recv()
        theirs = arrived[c]
        for i in range(GROUP):
            lanes = pl.ds(pl.multiple_of(c * LANES, LANES) + 128 * i, 128)
            both = jnp.concatenate([window[c, 128 * i : 128 * i + 128, :], theirs], axis=0)
            whole = dot(place[i], both, 1, 0).astype(BF16)
            for a in range(3):
                out_ref[a, :, :, lanes] = whole[:, 128 * a : 128 * a + 128].reshape(16, 8, 128)
        for copy in out_copies(c):
            copy.start()

    slot = x_lo * 4 + y
    copies = exchange(
        [(table_part.at[i], near_part.at[slot * 2 + core], near_send, near_recv, to) for i, to in near]
    )
    for copy in copies:
        copy.start()
    near_part[slot * 2 + core] = table_part[slot]
    gradients(CHUNKS - 2)
    gradients(CHUNKS - 1)
    for c in range(EARLY, CHUNKS):
        give_back(c)
    second_copy.wait()
    pre, cy, cx = hidden_before(layer_ref[0:2, :], layer_ref[2:3, :])
    hidden = jnp.maximum(pre, 0.0)
    hidden_ref[0], hidden_ref[1] = two_parts(hidden)
    sent = copies
    for copy in copies:
        copy.wait_recv()
    mine = near_part[0]
    for i in range(1, 16):
        mine = mine + near_part[i]

    z_part[z] = mine
    copies = exchange([(z_part.at[z], z_part.at[z], z_send, z_recv, to) for to in z_ids])
    for copy in copies:
        copy.start()

    for half in range(2):
        p = jax.nn.sigmoid(dot(seconds_ref[half], hidden, 1, 1, HIGHEST))
        slope_ref[half] = jnp.where(used_bins(HEADS), 16.0 * p * (1.0 - p), 0.0)

    @pl.loop(0, 2)
    def _(c):
        finish(c)

    sent = sent + copies
    for copy in copies:
        copy.wait_recv()
    mine = z_part[0]
    for i in range(1, 8):
        mine = mine + z_part[i]

    sums_ref[x * 4 + y] = mine
    here = sums_ref.at[x * 4 + y]
    copies = exchange([(here, here, xy_send, xy_recv, to) for to in xy_ids])
    for copy in copies:
        copy.start()

    @pl.loop(2, CHUNKS)
    def _(c):
        finish(c)

    @pl.loop(0, CHUNKS)
    def _(c):
        for side in range(2):
            in_copy(side, c).wait_send()
            back_copy(side, c).wait_send()

    seconds = jnp.concatenate([seconds_ref[0], seconds_ref[1]], axis=0)
    seconds_high, seconds_low = two_parts(seconds)
    seconds_three = jnp.concatenate([seconds_high, seconds_high, seconds_low], axis=0)
    sent = sent + copies
    for copy in copies:
        copy.wait_recv()

    def bins(half):
        strips = [
            jnp.concatenate([sums_ref[half * 8 + 2 * i], sums_ref[half * 8 + 2 * i + 1]], axis=1)
            for i in range(3)
        ]
        return jnp.concatenate(strips, axis=0)

    pulled = [bins(half)[0:HEADS] * slope_ref[half] for half in range(2)]
    high, low = two_parts(jnp.where(t == 0, pulled[0], pulled[1]))
    gsecond = dot(jnp.concatenate([high, low], axis=0), hidden_ref[0], 1, 0)
    gsecond_ref[...] = (
        gsecond[0:HEADS] + gsecond[HEADS : 2 * HEADS] + dot(high, hidden_ref[1], 1, 0)
    )
    high, low = two_parts(jnp.concatenate(pulled, axis=0))
    ghidden = dot(jnp.concatenate([high, low, high], axis=0), seconds_three, 0, 0)
    ghidden = jnp.where(pre > 0.0, ghidden, 0.0)
    gfirst_ref[0:1, :] = jnp.sum(cy * ghidden, axis=0, keepdims=True)
    gfirst_ref[1:2, :] = jnp.sum(cx * ghidden, axis=0, keepdims=True)
    goffset_ref[...] = jnp.sum(ghidden, axis=0, keepdims=True)
    r, n = iota((8, 256), 0), iota((8, 256), 1)
    pick = jnp.where(n == 24, jnp.where(r == 0, -1.0, 1.0), jnp.where((n == 8) & (r == 0), 1.0, 0.0))
    keys = dot(pick, jnp.where(t == 0, bins(0), bins(1)), 1, 1, HIGHEST)
    gkey_ref[...] = keys[0:2, 0:HEADS]
    for copy in sent:
        copy.wait_send()

    @pl.loop(0, CHUNKS)
    def _(c):
        for copy in out_copies(c):
            copy.wait()


def last_kernel(*refs):
    n = len(refs) // 3
    given, placed, held, sem = refs[:n], refs[n : 2 * n], refs[2 * n : 3 * n], refs[3 * n]
    pieces = [(i, pl.ds(4 * part, 4)) for part in range(4) for i in range(3)]
    pieces += [(i, slice(None)) for i in range(3, n)]
    loads, copies = [], []
    for at, (i, part) in enumerate(pieces):
        here = held[i].at[part]
        loads.append(pltpu.make_async_copy(given[i].at[part], here, sem.at[0, at]))
        copies.append(pltpu.make_async_copy(here, placed[i].at[part], sem.at[1, at]))
    for load in loads:
        load.start()
    for load, copy in zip(loads, copies):
        load.wait()
        copy.start()
    for copy in copies:
        copy.wait()


def on_device(q, k, v, d, land, shifts, first, offset, second, keybias):
    shape = q.shape
    field = (16, 8, HEADS * 128)
    fields = [a.reshape(field) for a in (q, k, v, d)]
    vmem = pl.BlockSpec(memory_space=pltpu.VMEM)
    hbm = pl.BlockSpec(memory_space=pltpu.HBM)
    dma = pltpu.SemaphoreType.DMA
    vec = pltpu.VMEM
    results = (jax.ShapeDtypeStruct(field, BF16),) * 3 + (
        jax.ShapeDtypeStruct((2, 512), F32),
        jax.ShapeDtypeStruct((1, 512), F32),
        jax.ShapeDtypeStruct((HEADS, 512), F32),
        jax.ShapeDtypeStruct((2, HEADS), F32),
    )
    outs = pl.pallas_call(
        main_kernel,
        out_shape=results,
        in_specs=[hbm] * 10,
        out_specs=(hbm,) * 3 + (vmem,) * 4,
        scratch_shapes=[
            vec((3,) + field, BF16),
            vec((16, 8, 128), F32),
            vec((2, HEADS, 512), F32),
            vec((3, 512), F32),
            vec((2, 256, 512), BF16),
            vec((2, HEADS, 256), F32),
            vec((2, GROUP, 128, 512), BF16),
            vec((2, GROUP, 128, 128), BF16),
            vec((2, GROUP, 128, 128), BF16),
            vec((4,) + field, BF16),
            vec((CHUNKS, GROUP * 128, 512), BF16),
            vec((CHUNKS, BOTH, 512), BF16),
            vec((CHUNKS, BOTH, 512), BF16),
            vec((CHUNKS, GROUP * 128, 384), BF16),
            vec((CHUNKS, BOTH, 384), BF16),
            vec((CHUNKS, BOTH, 384), BF16),
            vec((HEADS, 64, 128), F32),
            vec((1024, 256), BF16),
            vec((HEADS * 8, 128), F32),
            vec((HEADS * 8, 128), F32),
            vec((GROUP, 64, 128), F32),
            vec((BOTH, GROUP * 128), BF16),
            vec((BOTH, GROUP * 128), BF16),
            vec((GROUP, 128, 128 + BOTH), BF16),
            vec((GROUP, 128, 128 + BOTH), BF16),
            vec((8, 8, 128), F32),
            vec((16, 8, 128), F32),
            vec((8, 8, 128), F32),
            vec((16, 256), jnp.int32),
            vec((HEADS, 512), F32),
            pltpu.SMEM((2,), jnp.int32),
            pltpu.SMEM((2, HEADS), F32),
            dma((2, 4)),
            dma((6,)),
            dma((2, CHUNKS)),
            dma((2, CHUNKS)),
            dma((2, CHUNKS)),
            dma((2, CHUNKS)),
            dma((2,)),
            dma((15,)),
            dma((15,)),
            dma((7,)),
            dma((7,)),
            dma((15,)),
            dma((15,)),
            dma((3, CHUNKS)),
            pltpu.SemaphoreType.REGULAR((3,)),
        ],
        compiler_params=pltpu.CompilerParams(
            collective_id=0, has_side_effects=True, vmem_limit_bytes=60 * 2**20
        ),
        name="exchange_and_grads",
    )(*fields, land, shifts, first, offset.reshape(1, 512), second.T, keybias)
    gq, gk, gv, gfirst, goffset, gsecond, gkey = pl.pallas_call(
        last_kernel,
        out_shape=results,
        in_specs=[hbm] * 7,
        out_specs=(hbm,) * 7,
        scratch_shapes=[vec(r.shape, r.dtype) for r in results] + [dma((2, 16))],
        compiler_params=pltpu.CompilerParams(vmem_limit_bytes=60 * 2**20),
        name="write_and_reduce",
    )(*outs)
    return (
        gq.reshape(shape),
        gk.reshape(shape),
        gv.reshape(shape),
        gfirst,
        goffset.reshape(512),
        gsecond.T,
        gkey,
    )


def solution(mesh):
    field = P("dp", None, "space", "tensor")
    second = P(None, "tensor")
    return jax.shard_map(
        on_device,
        mesh=mesh,
        in_specs=(field,) * 4 + (P(), P(), P(), P(), second, second),
        out_specs=(field,) * 3 + (P(), P(), second, second),
        check_vma=False,
    )
```
